32 devices in a mesh: py: 4 (over z), pz: 8 (over y, x, core).
Axes of the slice: x: 2, y: 2, z: 4, core: 2. Of those that a mesh axis runs over, the one named last changes fastest.
Arguments:
- vort_p: bfloat16 [3, 131072], P(None, ('py', 'pz')), may hold values from -6 to 6
- pair_weights: bfloat16 [8192, 64, 128], P(('py', 'pz')), may hold values from -1.796875 to 1.796875
- pair_part: int32 [8192], P(('py', 'pz')), may hold values from 0 to 31
- pair_node: int32 [8192], P(('py', 'pz')), may hold values from 0 to 95, as said below
- counts: int32 [32], P(('py', 'pz')), may hold values from 128 to 256, as said below
Outputs:
- vel_p: float32 [3, 131072], P(None, ('py', 'pz'))
The draws below stay inside these ranges and needn't reach their ends.
Inputs may be any that keep to these rules, and one draw needn't show every extreme that they name: `counts`: every pencil has at least 128 live slots, and some pencil has all 256 slots live in every draw. `pair_node`: in every pencil the slots below 96 name each of its node blocks exactly once.
All inputs are finite; a program needn't handle non-finite values.
Results may differ from the reference program's by a relative error of at most 0.0029.
Values sent between devices are 32-bit elements; how exact they have to be, the bound alone decides.
A program may use at most 64 MiB of HBM per device.

```python
import math
import jax
import jax.numpy as jnp
from jax import lax

NX = 384
CY = 8
CZ = 2
BP = 128
BN = 64
PB_DEV = 32
PAIR_DEV = 256
NB_DEV = 96
PENCILS = 32
PARTS_SIZE = 131072
PAIRS = 8192
NY = 32
NZ = 16
N_PY = 4
N_PZ = 8


def draw_counts(key, part):
    first, second, third = jax.random.split(key, 3)
    spread_top = PAIR_DEV - PAIR_DEV // 2
    draw_one = jax.random.randint(first, (PENCILS,), 0, spread_top + 1)
    draw_two = jax.random.randint(second, (PENCILS,), 0, spread_top + 1)
    base = PAIR_DEV // 2 + jnp.minimum(draw_one, draw_two)
    busiest = jax.random.randint(third, (), 0, PENCILS)
    return jnp.where(jnp.arange(PENCILS) == busiest, PAIR_DEV, base).astype(jnp.int32)


def draw_pair_node(key, part):
    order_key, rest_key = jax.random.split(jax.random.fold_in(key, 17))
    pencil_keys = jax.random.split(order_key, PENCILS)
    covering = jax.vmap(lambda one_key: jax.random.permutation(one_key, NB_DEV))(pencil_keys).astype(jnp.int32)
    others = jax.random.randint(rest_key, (PENCILS, PAIR_DEV - NB_DEV), 0, NB_DEV).astype(jnp.int32)
    return jnp.concatenate([covering, others], axis=1).reshape(PENCILS * PAIR_DEV)


def plant(drawn, own_key, least, high):
    extent = drawn.shape
    index_at = [jax.random.randint(jax.random.fold_in(own_key, axis), (), 0, extent[axis]) for axis in range(len(extent))]
    drawn = drawn.at[tuple(index_at)].set(least)
    longest = extent.index(max(extent))
    index_at[longest] = (index_at[longest] + 1) % extent[longest]
    return drawn.at[tuple(index_at)].set(high)


def levels(own_key, shape, cuts, least, top_value):
    loudness, own = 1.0, jax.random.fold_in(own_key, 6)
    for dim, blocks in cuts:
        heights = jnp.exp(jax.random.uniform(jax.random.fold_in(own, dim), (blocks,), jnp.float32, least / len(cuts), top_value / len(cuts)))
        loudness = loudness * jnp.repeat(heights, shape[dim] // blocks).reshape([-1 if axis == dim else 1 for axis in range(len(shape))])
    return loudness


def bell_draw(rng, shape, deviation, limit, pieces=(), dtype=jnp.bfloat16):
    result = jax.random.normal(rng, shape, jnp.float32) * deviation
    if len(pieces) > 0:
        result = levels(rng, shape, pieces, -0.22, 0.18) * result
    return jnp.clip(result, min=-limit, max=limit).astype(dtype)


def setup_inputs(seed: int = 0) -> dict:
    key_list = jax.random.split(jax.random.key(seed), 6)
    return {
        "vort_p": bell_draw(key_list[0], (3, PARTS_SIZE), 1.0, 6.0, ((1, 32),)),
        "pair_weights": bell_draw(key_list[1], (PAIRS, BN, BP), 0.3, 1.796875, ((0, 32),)),
        "pair_part": plant(jax.random.randint(key_list[2], (PAIRS,), 0, PB_DEV), jax.random.fold_in(key_list[2], 1), 0, PB_DEV - 1).astype(jnp.int32),
        "pair_node": draw_pair_node(jax.random.fold_in(key_list[5], 71), 0),
        "counts": draw_counts(jax.random.fold_in(key_list[5], 71), 0),
    }


def cross_terms(coeffs, field):
    return jnp.stack([coeffs[1] * field[2] - coeffs[2] * field[1], coeffs[2] * field[0] - coeffs[0] * field[2], coeffs[0] * field[1] - coeffs[1] * field[0]], axis=0)


def signed_wave(length, count):
    index = jnp.arange(count)
    signed = jnp.where(index < length // 2, index, index - length)
    return signed.astype(jnp.float32) * (2.0 * math.pi / length), index == length // 2


def reference(vort_p, pair_weights, pair_part, pair_node, counts):
    node_blocks = NX * CY * CZ // BN
    particle_blocks = vort_p.reshape(3, PENCILS, PB_DEV, BP).transpose(1, 2, 0, 3)
    tile_weights = pair_weights.reshape(PENCILS, PAIR_DEV, BN, BP)
    part_index = pair_part.reshape(PENCILS, PAIR_DEV)
    node_index = pair_node.reshape(PENCILS, PAIR_DEV)

    def spread(inputs):
        blocks, weights, parts, nodes, count = inputs
        picked = blocks[parts].astype(jnp.float32)
        products = jnp.einsum('pcq,pnq->pcn', picked, weights.astype(jnp.float32))
        live_mask = (jnp.arange(PAIR_DEV) < count).astype(jnp.float32)
        products = products * live_mask[:, None, None]
        return jax.ops.segment_sum(products, nodes, num_segments=node_blocks)

    local_nodes = lax.map(spread, (particle_blocks, tile_weights, part_index, node_index, counts))
    vort_grid = local_nodes.transpose(0, 2, 1, 3).reshape(N_PY, N_PZ, 3, CZ, CY, NX)
    vort_grid = vort_grid.transpose(2, 1, 3, 0, 4, 5).reshape(3, NZ, NY, NX)
    vort_hat = jnp.fft.rfftn(vort_grid, axes=(1, 2, 3))
    x_modes = NX // 2 + 1
    wave_z, edge_z = signed_wave(NZ, NZ)
    wave_y, edge_y = signed_wave(NY, NY)
    mode_x = jnp.arange(x_modes)
    wave_x = mode_x.astype(jnp.float32) * (2.0 * math.pi / NX)
    edge_x = mode_x == NX // 2
    wave_x3 = wave_x[None, None, :]
    wave_y3 = wave_y[None, :, None]
    wave_z3 = wave_z[:, None, None]
    total = wave_x3 * wave_x3 + wave_y3 * wave_y3 + wave_z3 * wave_z3
    edges = edge_z[:, None, None] | edge_y[None, :, None] | edge_x[None, None, :]
    keep = (total > 0) & jnp.logical_not(edges)
    inverse_sq = jnp.where(keep, 1.0 / jnp.where(keep, total, 1.0), 0.0)
    inv_wave = (wave_x3 * inverse_sq, wave_y3 * inverse_sq, wave_z3 * inverse_sq)
    vel_hat = 1j * cross_terms(inv_wave, vort_hat)
    vel_grid = jnp.fft.irfftn(vel_hat, s=(NZ, NY, NX), axes=(1, 2, 3)).astype(jnp.bfloat16)
    vel_nodes = vel_grid.reshape(3, N_PZ, CZ, N_PY, CY, NX).transpose(3, 1, 0, 2, 4, 5)
    vel_nodes = vel_nodes.reshape(PENCILS, 3, node_blocks, BN).transpose(0, 2, 1, 3)

    def collect(inputs):
        nodes_vel, weights, parts, nodes, count = inputs
        picked = nodes_vel[nodes].astype(jnp.float32)
        products = jnp.einsum('pcn,pnq->pcq', picked, weights.astype(jnp.float32))
        live_mask = (jnp.arange(PAIR_DEV) < count).astype(jnp.float32)
        products = products * live_mask[:, None, None]
        return jax.ops.segment_sum(products, parts, num_segments=PB_DEV)

    per_block = lax.map(collect, (vel_nodes, tile_weights, part_index, node_index, counts))
    return per_block.transpose(2, 0, 1, 3).reshape(3, PARTS_SIZE)
```

```python
import functools
import math

import jax
import jax.numpy as jnp
import numpy as np
from jax import lax
from jax.experimental import pallas as pl
from jax.experimental.pallas import tpu as pltpu
from jax.sharding import PartitionSpec as P

NX = 384
CY = 8
CZ = 2
BP = 128
BN = 64
PB_DEV = 32
ROWS = 8
CHUNK = 32
GROUP = 4
N_PY = 4
N_PZ = 8
MESH = pl.DeviceIdType.MESH
f32 = jnp.float32
bf16 = jnp.bfloat16


def twiddle(row_index, col_index, period):
    product = row_index[:, None] * col_index[None, :] % period
    return product.astype(jnp.float32) * (2.0 * math.pi / period)


def forward_table(length):
    angle = twiddle(jnp.arange(length), jnp.arange(length), length)
    cosine = jnp.cos(angle)
    sines = jnp.sin(angle)
    return jnp.stack([jnp.stack([cosine, -sines], 1), jnp.stack([sines, cosine], 1)], 0)


def inverse_table(length):
    angle = twiddle(jnp.arange(length), jnp.arange(length), length)
    cosine = jnp.cos(angle) / length
    sines = jnp.sin(angle) / length
    return jnp.stack([jnp.stack([cosine, sines], 1), jnp.stack([-sines, cosine], 1)], 0)


def cross_terms(coeffs, field):
    return jnp.stack(
        [
            coeffs[1] * field[2] - coeffs[2] * field[1],
            coeffs[2] * field[0] - coeffs[0] * field[2],
            coeffs[0] * field[1] - coeffs[1] * field[0],
        ],
        axis=0,
    )


def signed_wave(length, index):
    signed = jnp.where(index < length // 2, index, index - length)
    return (signed.astype(jnp.float32) * (2.0 * math.pi / length), index == length // 2)


def curl_solve(spectrum, y_cells, z_cells):
    x_local = spectrum.shape[1]
    y_local = spectrum.shape[3]
    mode_x = lax.axis_index("py") * x_local + jnp.arange(x_local)
    wave_x = mode_x.astype(jnp.float32) * (2.0 * math.pi / NX)
    wave_y, edge_y = signed_wave(y_cells, lax.axis_index("pz") * y_local + jnp.arange(y_local))
    wave_z, edge_z = signed_wave(z_cells, jnp.arange(z_cells))
    wave_x3 = wave_x[:, None, None]
    wave_y3 = wave_y[None, :, None]
    wave_z3 = wave_z[None, None, :]
    total = wave_x3 * wave_x3 + wave_y3 * wave_y3 + wave_z3 * wave_z3
    edges = edge_y[None, :, None] | edge_z[None, None, :]
    keep = (total > 0) & jnp.logical_not(edges)
    inverse_sq = jnp.where(keep, 1.0 / jnp.where(keep, total, 1.0), 0.0)
    inv_wave = (wave_x3 * inverse_sq, wave_y3 * inverse_sq, wave_z3 * inverse_sq)
    real_turn = cross_terms(inv_wave, spectrum[:, :, 0])
    imag_turn = cross_terms(inv_wave, spectrum[:, :, 1])
    return jnp.stack([-imag_turn, real_turn], axis=2)


def halves(table):
    table = np.asarray(table, np.float32)
    high = table.astype(bf16)
    return high, (table - high.astype(np.float32)).astype(bf16)


def split(x):
    high = x.astype(bf16)
    return high, (x - high.astype(f32)).astype(bf16)


def dot(a, b, dims=((1,), (0,))):
    return lax.dot_general(a, b, (dims, ((), ())), preferred_element_type=f32)


def left_half(shape):
    return lax.broadcasted_iota(jnp.int32, shape, 1) < BN


def spread_kernel(part, node, count, parts_ref, w_ref, out_ref, near_ref, parts, sems):
    chunks = w_ref.shape[0] // CHUNK

    def fetch(k):
        here = pl.ds(k * CHUNK, CHUNK)
        return pltpu.make_async_copy(w_ref.at[here], near_ref.at[here], sems.at[k])

    for k in range(chunks):
        fetch(k).start()
    out_ref[...] = jnp.zeros_like(out_ref)
    parts[...] = jnp.zeros_like(parts)
    for b in range(PB_DEV):
        parts[b, 0:3, :] = parts_ref[:, b * BP : (b + 1) * BP].astype(f32)
    left = left_half((ROWS, 128))

    def chunk(k, carry):
        fetch(k).wait()
        base = k * CHUNK
        for g in range(CHUNK // GROUP):
            first = base + g * GROUP
            picked = jnp.concatenate([parts[part[first + i]] for i in range(GROUP)], axis=0)
            tiles = near_ref[pl.ds(first, GROUP)].reshape(GROUP * BN, BP)
            got = dot(picked.astype(bf16), tiles, ((1,), (1,)))
            for i in range(GROUP):
                keep = jnp.logical_and(left if i % 2 == 0 else ~left, first + i < count[0])
                lanes = i // 2 * 128
                own = got[i * ROWS : (i + 1) * ROWS, lanes : lanes + 128]
                out_ref[node[first + i]] += jnp.where(keep, own, 0.0)
        return carry

    lax.fori_loop(0, chunks, chunk, 0)


def spread(vort_p, weights, part, node, counts, node_blocks):
    smem = pl.BlockSpec(memory_space=pltpu.SMEM)
    vmem = pl.BlockSpec(memory_space=pltpu.VMEM)
    return pl.pallas_call(
        spread_kernel,
        out_shape=(
            jax.ShapeDtypeStruct((node_blocks, ROWS, 2 * BN), f32),
            jax.ShapeDtypeStruct(weights.shape, weights.dtype),
        ),
        in_specs=[smem, smem, smem, vmem, pl.BlockSpec(memory_space=pltpu.HBM)],
        out_specs=(vmem, vmem),
        scratch_shapes=[
            pltpu.VMEM((PB_DEV, ROWS, BP), f32),
            pltpu.SemaphoreType.DMA((weights.shape[0] // CHUNK,)),
        ],
        compiler_params=pltpu.CompilerParams(vmem_limit_bytes=48 * 2**20),
        name="spread",
    )(part, node, counts, vort_p, weights)


def collect_kernel(part, node, count, vel_ref, w_ref, out_ref, sums):
    sums[...] = jnp.zeros_like(sums)
    left = left_half((ROWS, 128))
    zero = jnp.zeros((ROWS, 128), f32)

    def chunk(k, carry):
        for g in range(CHUNK // GROUP):
            first = k * CHUNK + g * GROUP
            rows = []
            for i in range(GROUP):
                slot = first + i
                keep = jnp.logical_and(left if i % 2 == 0 else ~left, slot < count[0])
                own = jnp.where(keep, vel_ref[node[slot]], 0.0)
                rows.append(
                    jnp.concatenate(
                        [own if h == i // 2 else zero for h in range(GROUP // 2)], axis=1
                    )
                )
            chosen = jnp.concatenate(rows, axis=0).astype(bf16)
            got = dot(chosen, w_ref[pl.ds(first, GROUP)].reshape(GROUP * BN, BP))
            for i in range(GROUP):
                sums[part[first + i]] += got[i * ROWS : (i + 1) * ROWS]
        return carry

    lax.fori_loop(0, w_ref.shape[0] // CHUNK, chunk, 0)
    for b in range(PB_DEV):
        out_ref[:, b * BP : (b + 1) * BP] = sums[b, 0:3, :]


def collect(vel, weights, part, node, counts):
    smem = pl.BlockSpec(memory_space=pltpu.SMEM)
    vmem = pl.BlockSpec(memory_space=pltpu.VMEM)
    return pl.pallas_call(
        collect_kernel,
        out_shape=jax.ShapeDtypeStruct((3, PB_DEV * BP), f32),
        in_specs=[smem, smem, smem, vmem, vmem],
        out_specs=vmem,
        scratch_shapes=[pltpu.VMEM((PB_DEV, ROWS, BP), f32)],
        compiler_params=pltpu.CompilerParams(vmem_limit_bytes=24 * 2**20),
        name="collect",
    )(part, node, counts, vel, weights)


def tables():
    devices = N_PY * N_PZ
    local = NX // 2 // devices
    ny, nz = CY * N_PY, CZ * N_PZ
    row = np.arange(devices * ROWS)
    slot, device = row % ROWS, row // ROWS
    mode = device * local + slot
    angle = 2 * np.pi * (mode[:, None] * np.arange(NX)[None] % NX) / NX
    used = (slot < local)[:, None]
    x_cos, x_sin = np.where(used, np.cos(angle), 0.0), np.where(used, -np.sin(angle), 0.0)
    index = np.arange(devices)
    a, b = index // N_PZ, index % N_PZ
    lane = np.arange(128)
    real, comp, cell = lane // 64, lane % 64 // 16, lane % 16
    zl, yl = cell // CY, cell % CY
    valid = (comp < 3)[None]
    phi = 2 * np.pi * (a[:, None] * yl[None] / ny + b[:, None] * zl[None] / nz)
    sign = np.where(real == 0, 1.0, -1.0)[None]
    turn_cos, turn_sin = np.cos(phi), np.sin(phi) * sign
    psi = 2 * np.pi * (yl[:, None] * yl[None] / CY + zl[:, None] * zl[None] / CZ)
    cosine, sines = np.cos(psi), np.sin(psi)
    r, q = real[:, None], real[None]

    def near(ahead):
        both = np.where(r == q, sines, np.where(r == 0, cosine, -cosine))
        same = (comp[:, None] == (comp[None] + ahead) % 3) & (comp[:, None] < 3) & valid
        return np.where(same, both, 0.0)

    forward = np.concatenate([near(2), near(1)], 1)
    both = np.where(r == q, cosine, np.where(r == 0, sines, -sines))
    same = (comp[:, None] == comp[None]) & (comp[:, None] < 3)
    back = np.where(same, both, 0.0)
    my, mz = a[:, None] + N_PY * yl[None], b[:, None] + N_PZ * zl[None]
    keep = (my != ny // 2) & (mz != nz // 2) & valid
    my, mz = np.where(my < ny // 2, my, my - ny), np.where(mz < nz // 2, mz, mz - nz)
    ky, kz = 2 * np.pi * my / ny, 2 * np.pi * mz / nz
    zero = np.zeros_like(ky)
    wave = np.stack([zero, ky, kz])
    k_first = np.where(comp == 0, wave[1], np.where(comp == 1, wave[2], wave[0]))
    k_second = np.where(comp == 0, wave[2], np.where(comp == 1, wave[0], wave[1]))
    x_first = np.broadcast_to(comp == 2, ky.shape)
    x_second = np.broadcast_to(comp == 1, ky.shape)
    small = [turn_cos, turn_sin, ky * ky + kz * kz, k_first, k_second, x_first, x_second, keep]
    small = np.stack(small).astype(np.float32)
    near_table = np.concatenate([forward, back], 1)
    near_high = near_table.astype(np.float32).astype(bf16)
    return [
        *halves(np.concatenate([x_cos, x_sin], 1)),
        np.concatenate([near_high, near_high], 0),
        small,
    ]


def flip(index, bits):
    for bit in (1, 2, 4):
        if bits & bit:
            index = index + bit - 2 * bit * (index // bit % 2)
    return index


def swap(x):
    return pltpu.roll(x, 64, 1)


def line_transform(x, turn):
    if len(x) == 2:
        return [x[0] + x[1], x[0] - x[1]]
    half = len(x) // 2
    even = [x[k] + x[k + half] for k in range(half)]
    odd = [x[k] - x[k + half] for k in range(half)]
    if half == 2:
        side = turn(odd[1])
        low, high = line_transform(even, turn), [odd[0] + side, odd[0] - side]
    else:
        side = turn(odd[2])
        near, far = odd[1] - odd[3], turn(odd[1] + odd[3])
        root = math.sqrt(0.5)
        plus, minus = (near + far) * root, (far - near) * root
        first, second = odd[0] + side, odd[0] - side
        low = line_transform(even, turn)
        high = [first + plus, second + minus, first - plus, second - minus]
    return [value for pair in zip(low, high) for value in pair]


def plane_transform(blocks, turn):
    columns = [
        line_transform([blocks[a * N_PZ + b] for a in range(N_PY)], turn) for b in range(N_PZ)
    ]
    lines = [line_transform([columns[b][a] for b in range(N_PZ)], turn) for a in range(N_PY)]
    return [lines[a][b] for a in range(N_PY) for b in range(N_PZ)]


def solve_kernel(
    count,
    part_hbm,
    node_hbm,
    parts_hbm,
    w_ref,
    xh_hbm,
    xl_hbm,
    near_hbm,
    small_hbm,
    near_ref,
    vel_ref,
    choose_ref,
    gather_ref,
    part_ref,
    node_ref,
    parts_ref,
    xh_ref,
    xl_ref,
    tab_ref,
    small,
    send_a,
    recv_a,
    send_b,
    recv_b,
    send_sem,
    recv_sem,
    parts,
    picks,
    pairs,
    held,
    sems,
    const_sems,
    first_sems,
):
    devices = N_PY * N_PZ
    local = NX // 2 // devices
    rows = devices * ROWS
    per_row = NX // BN
    cells = CY * CZ
    groups = w_ref.shape[1]
    slots = GROUP * groups
    chunks = sems.shape[0]
    step = groups // chunks
    my_y, my_z = lax.axis_index("py"), lax.axis_index("pz")
    me = my_y * N_PZ + my_z
    others = [
        (flip(my_y, ky), flip(my_z, kz))
        for ky in (2, 3, 1, 0)
        for kz in range(N_PZ - 1, -1, -1)
        if ky or kz
    ]

    def fetch(k):
        here = pl.ds(k * step, step)
        return pltpu.make_async_copy(w_ref.at[:, here], near_ref.at[:, here], sems.at[k])

    firsts = [
        pltpu.make_async_copy(c, h, first_sems.at[i])
        for i, (c, h) in enumerate(
            ((parts_hbm, parts_ref), (part_hbm, part_ref), (node_hbm, node_ref))
        )
    ]
    for load in firsts:
        load.start()
    for k in range(chunks):
        fetch(k).start()
    if not False:
        barrier = pltpu.get_barrier_semaphore()
        for other in others:
            pl.semaphore_signal(barrier, inc=1, device_id=other, device_id_type=MESH)
    loads = [
        pltpu.make_async_copy(c, h, const_sems.at[i])
        for i, (c, h) in enumerate(
            ((xh_hbm, xh_ref), (xl_hbm, xl_ref), (near_hbm, tab_ref), (small_hbm, small))
        )
    ]
    for load in loads:
        load.start()

    sent = pl.ds(0, local)

    def exchange(send, recv, phase):
        if False:
            recv[...] = send[...]
            return
        for to_y, to_z in others:
            pltpu.make_async_remote_copy(
                src_ref=send.at[to_y * N_PZ + to_z, sent],
                dst_ref=recv.at[me, sent],
                send_sem=send_sem.at[phase],
                recv_sem=recv_sem.at[phase],
                device_id=(to_y, to_z),
                device_id_type=MESH,
            ).start()

    def wait_all(buffer, sem):
        if False:
            return
        many = pl.ds(0, devices - 1)
        pltpu.make_async_copy(buffer.at[many, sent], buffer.at[many, sent], sem).wait()

    def stop(value):
        vel_ref[...] = jnp.zeros_like(vel_ref) + value.astype(bf16)
        choose_ref[...] = jnp.zeros_like(choose_ref)
        gather_ref[...] = jnp.zeros_like(gather_ref)

    def wait_fetches():
        for k in range(chunks):
            fetch(k).wait()
        for load in loads:
            load.wait()

    for load in firsts:
        load.wait()
    if 0 == 1:
        wait_fetches()
        return stop(jnp.zeros((1, 128), f32))

    for b in range(PB_DEV):
        parts[b * ROWS : b * ROWS + 3, :] = parts_ref[:, b * BP : (b + 1) * BP].astype(f32)
    row = lax.broadcasted_iota(jnp.int32, (PB_DEV, slots), 0)
    chooser = jnp.where(row == part_ref[...], 1.0, 0.0).T.astype(bf16)
    tall = GROUP * 4
    for c in range(3):
        block = parts[pl.ds(c, PB_DEV, stride=ROWS), :].astype(bf16)
        got = dot(chooser, block)
        for i in range(GROUP):
            here = pl.ds(c * GROUP + i, groups, stride=tall)
            picks[here, :] = got[i * groups : (i + 1) * groups]
    if 0 == 2:
        wait_fetches()
        return stop(picks[0:1])
    if 0 == 3:
        wait_fetches()
    sub = lax.broadcasted_iota(jnp.int32, (tall, 128), 0) % GROUP
    half = lax.broadcasted_iota(jnp.int32, (tall, 128), 1) // BN
    low_slots = sub < 2
    own_half = sub % 2 == half
    for k in range(chunks):
        if 0 != 3:
            fetch(k).wait()
        for g in range(k * step, (k + 1) * step):
            picked = picks[g * tall : (g + 1) * tall, :].astype(bf16)
            tiles = near_ref[:, g].reshape(GROUP * BN, BP)
            got = dot(picked, tiles, ((1,), (1,)))
            own = jnp.where(low_slots, got[:, :128], got[:, 128:])
            pairs[g * tall : (g + 1) * tall, :] = jnp.where(own_half, own, 0.0)
    if 0 != 3:
        for load in loads:
            load.wait()
    if 0 == 3 or 0 == 4:
        return stop(pairs[0:1])

    def pairs_of(c):
        return jnp.concatenate(
            [pairs[pl.ds(c * GROUP + i, groups, stride=tall), :] for i in range(GROUP)], axis=0
        )

    row = lax.broadcasted_iota(jnp.int32, (cells * per_row, slots), 0)
    block = row % cells * per_row + row // cells
    live = lax.broadcasted_iota(jnp.int32, (cells * per_row, slots), 1) < count[0]
    hits = jnp.where((block == node_ref[...]) & live, 1.0, 0.0)
    choose_ref[...] = hits.T.astype(bf16)
    hits = hits.astype(bf16)
    left = left_half((cells, 128))
    lines = []
    for c in range(3):
        total = dot(hits, jnp.concatenate(split(pairs_of(c)), axis=1))
        total = total[:, :128] + total[:, 128:]
        total += swap(total)
        pieces = [
            jnp.where(
                left, total[xb * cells : (xb + 1) * cells], total[(xb + 1) * cells : (xb + 2) * cells]
            )
            for xb in range(0, per_row, 2)
        ]
        lines.append(jnp.concatenate(pieces, axis=1))
    vort = jnp.concatenate([*lines, jnp.zeros((cells, NX), f32)], axis=0)
    if 0 == 5:
        return stop(vort[0:1, 0:128])
    high, rest = split(vort)
    none = jnp.zeros_like(high)
    both = [
        jnp.concatenate(
            [jnp.concatenate([x, none], axis=1), jnp.concatenate([none, x], axis=1)], axis=0
        )
        for x in (high, rest)
    ]
    over = ((1,), (1,))
    modes = dot(xh_ref[...], jnp.concatenate(both, axis=0), over)
    modes = modes[:, :128] + (modes[:, 128:] + dot(xl_ref[...], both[0], over))
    send_a[...] = modes.reshape(devices, ROWS, 128)
    recv_a[me] = send_a[me]
    if 0 == 6:
        return stop(send_a[0, 0:1])
    if not False:
        pl.semaphore_wait(barrier, devices - 1)
    exchange(send_a, recv_a, 0)

    unsent = jnp.zeros((devices, ROWS - local, 128), f32)
    recv_b[:, local:, :] = unsent
    row = lax.broadcasted_iota(jnp.int32, (PB_DEV, slots), 0)
    live = lax.broadcasted_iota(jnp.int32, (PB_DEV, slots), 1) < count[0]
    gather_ref[...] = jnp.where((row == part_ref[...]) & live, 1.0, 0.0).astype(bf16)

    def spread_out(i):
        return jnp.broadcast_to(small[i][:, None, :], (devices, ROWS, 128)).reshape(rows, 128)

    slot = lax.broadcasted_iota(jnp.int32, (rows, 128), 0) % ROWS
    mode = me * local + slot
    wave_x = mode.astype(f32) * (2.0 * math.pi / NX)
    total = spread_out(2) + wave_x * wave_x
    weight = jnp.where(mode == 0, 1.0, 2.0) * (1.0 / (NX * CY * N_PY * CZ * N_PZ))
    inverse = spread_out(7) * weight / jnp.where(total > 0, total, 1.0)
    held[0] = (spread_out(3) + wave_x * spread_out(5)) * inverse
    held[1] = (spread_out(4) + wave_x * spread_out(6)) * inverse
    held[2], held[3] = spread_out(0), spread_out(1)
    sign = jnp.where(lax.broadcasted_iota(jnp.int32, (ROWS, 128), 1) < 64, 1.0, -1.0)

    def ahead(x):
        return swap(x) * sign

    def astern(x):
        return swap(x) * -sign

    def along(x, table):
        return dot(jnp.concatenate(split(x), axis=1), table)

    wait_all(recv_a, recv_sem.at[0])
    if 0 == 7:
        return stop(recv_a[0, 0:1] + held[0, 0:1] + held[1, 0:1] + held[2, 0:1] + held[3, 0:1])
    y = plane_transform([recv_a[d] for d in range(devices)], ahead)
    y = jnp.concatenate(y, axis=0)
    if 0 == 8:
        send_b[...] = y.reshape(devices, ROWS, 128)
        return stop(send_b[0, 0:1])
    z = held[2] * y + held[3] * swap(y)
    both = along(z, tab_ref[:, 0:256])
    if 0 == 9:
        send_b[...] = (both[:, :128] + both[:, 128:]).reshape(devices, ROWS, 128)
        return stop(send_b[0, 0:1])
    vel = held[0] * both[:, :128] - held[1] * both[:, 128:]
    y = along(vel, tab_ref[:, 256:384])
    z = held[2] * y - held[3] * swap(y)
    if 0 == 10:
        send_b[...] = z.reshape(devices, ROWS, 128)
        return stop(send_b[0, 0:1])
    z = plane_transform([z[d * ROWS : (d + 1) * ROWS] for d in range(devices)], astern)
    for d in range(devices):
        send_b[d] = z[d]
    recv_b[me, 0:local] = send_b[me, 0:local]
    if 0 == 11:
        return stop(send_b[0, 0:1])
    exchange(send_b, recv_b, 1)
    wait_all(send_a, send_sem.at[0])
    wait_all(recv_b, recv_sem.at[1])
    back = recv_b[...].reshape(rows, 128).T
    grid = jnp.zeros((48, NX), f32)
    for k in range(2):
        high, rest = split(back[64 * k : 64 * k + 48])
        table = xh_ref[:, k * NX : (k + 1) * NX]
        both = dot(jnp.concatenate([high, rest], axis=0), table)
        grid += both[:48] + (both[48:] + dot(high, xl_ref[:, k * NX : (k + 1) * NX]))
    if 0 == 12:
        return stop(grid[0:1, 0:128])
    for c in range(3):
        for xb in range(0, per_row, 2):
            piece = grid[c * cells : (c + 1) * cells, xb * BN : (xb + 2) * BN]
            other = swap(piece)
            for h, line in ((0, jnp.where(left, piece, other)), (1, jnp.where(left, other, piece))):
                vel_ref[c, (xb + h) * cells : (xb + h + 1) * cells, :] = line.astype(bf16)
    wait_all(send_b, send_sem.at[1])


def collect_kernel_b(vel_ref, choose_ref, gather_ref, w_ref, out_ref, picks, pairs, sums):
    groups = w_ref.shape[1]
    tall = GROUP * 4
    picks[...] = jnp.zeros_like(picks)
    chooser = choose_ref[...]
    for c in range(3):
        got = dot(chooser, vel_ref[c])
        for i in range(GROUP):
            here = pl.ds(c * GROUP + i, groups, stride=tall)
            picks[here, :] = got[i * groups : (i + 1) * groups]
    sub = lax.broadcasted_iota(jnp.int32, (tall, 128), 0) % GROUP
    half = lax.broadcasted_iota(jnp.int32, (tall, 128), 1) // BN
    first = (sub < 2) & (sub % 2 == half)
    second = (sub >= 2) & (sub % 2 == half)
    for g in range(groups):
        line = picks[g * tall : (g + 1) * tall, :]
        chosen = jnp.concatenate([jnp.where(first, line, 0.0), jnp.where(second, line, 0.0)], axis=1)
        pairs[g * tall : (g + 1) * tall, :] = dot(
            chosen.astype(bf16), w_ref[:, g].reshape(GROUP * BN, BP)
        )
    for c in range(3):
        lines = jnp.concatenate(
            [pairs[pl.ds(c * GROUP + i, groups, stride=tall), :] for i in range(GROUP)], axis=0
        )
        total = dot(gather_ref[...], jnp.concatenate(split(lines), axis=1))
        sums[pl.ds(c, PB_DEV, stride=ROWS), :] = total[:, :128] + total[:, 128:]
    for b in range(PB_DEV):
        out_ref[:, b * BP : (b + 1) * BP] = sums[b * ROWS : b * ROWS + 3, :]


def solve_direct(vort_p, weights, part, node, counts):
    devices = N_PY * N_PZ
    node_blocks = NX * CY * CZ // BN
    slots = weights.shape[0]
    groups = slots // GROUP
    vmem = pl.BlockSpec(memory_space=pltpu.VMEM)
    hbm = pl.BlockSpec(memory_space=pltpu.HBM)
    block = pltpu.VMEM((devices, ROWS, 128), f32)
    consts = [jnp.asarray(t) for t in tables()]
    weights = weights.reshape(GROUP, groups, BN, BP)
    inputs = [part[None], node[None], vort_p, weights, *consts]
    tall = pltpu.VMEM((groups * GROUP * 4, 128), f32)
    near, vel, chooser, gather = pl.pallas_call(
        solve_kernel,
        out_shape=(
            jax.ShapeDtypeStruct(weights.shape, weights.dtype),
            jax.ShapeDtypeStruct((3, node_blocks, 128), bf16),
            jax.ShapeDtypeStruct((slots, node_blocks), bf16),
            jax.ShapeDtypeStruct((PB_DEV, slots), bf16),
        ),
        in_specs=[pl.BlockSpec(memory_space=pltpu.SMEM)] + [hbm] * len(inputs),
        out_specs=(vmem, vmem, vmem, vmem),
        scratch_shapes=[
            pltpu.VMEM((1, slots), jnp.int32),
            pltpu.VMEM((1, slots), jnp.int32),
            pltpu.VMEM(vort_p.shape, vort_p.dtype),
            *[pltpu.VMEM(t.shape, t.dtype) for t in consts],
            block,
            block,
            block,
            block,
            pltpu.SemaphoreType.DMA((2,)),
            pltpu.SemaphoreType.DMA((2,)),
            pltpu.VMEM((PB_DEV * ROWS, BP), f32),
            tall,
            tall,
            pltpu.VMEM((4, devices * ROWS, 128), f32),
            pltpu.SemaphoreType.DMA((8,)),
            pltpu.SemaphoreType.DMA((len(consts),)),
            pltpu.SemaphoreType.DMA((3,)),
        ],
        compiler_params=pltpu.CompilerParams(
            collective_id=None if False else 0, has_side_effects=True, vmem_limit_bytes=24 * 2**20
        ),
        name="solve",
    )(counts, *[pltpu.with_memory_space_constraint(x, pltpu.HBM) for x in inputs])
    return pl.pallas_call(
        collect_kernel_b,
        out_shape=jax.ShapeDtypeStruct((3, PB_DEV * BP), f32),
        in_specs=[vmem] * 4,
        out_specs=vmem,
        scratch_shapes=[tall, tall, pltpu.VMEM((PB_DEV * ROWS, BP), f32)],
        compiler_params=pltpu.CompilerParams(vmem_limit_bytes=16 * 2**20),
        name="collect_last",
    )(vel, chooser, gather, near)


def solve_staged(sums, n_py, n_pz):
    highest = lax.Precision.HIGHEST
    node_blocks = sums.shape[0]
    y_cells, z_cells = CY * n_py, CZ * n_pz
    x_modes = NX // 2
    sums = sums[:, :3, :BN] + sums[:, :3, BN:]
    vort_grid = sums.transpose(1, 0, 2).reshape(3, CZ, CY, NX)
    angle_fwd = twiddle(jnp.arange(NX), jnp.arange(x_modes), NX)
    x_forward = jnp.stack([jnp.cos(angle_fwd), -jnp.sin(angle_fwd)], 1)
    angle_inv = twiddle(jnp.arange(x_modes), jnp.arange(NX), NX)
    mode_weight = (jnp.where(jnp.arange(x_modes) == 0, 1.0, 2.0) / NX)[:, None]
    x_inverse = jnp.stack([mode_weight * jnp.cos(angle_inv), -mode_weight * jnp.sin(angle_inv)], 0)
    y_forward = forward_table(y_cells)
    z_forward = forward_table(z_cells)
    z_inverse = inverse_table(z_cells)
    y_inverse = inverse_table(y_cells)
    x_spectrum = jnp.einsum("czyx,xrm->czrmy", vort_grid, x_forward, precision=highest)
    row_section = jnp.einsum(
        "czrmy,rysk->cmskz",
        lax.all_to_all(x_spectrum, "py", split_axis=3, concat_axis=4, tiled=True),
        y_forward,
        precision=highest,
    )
    col_section = jnp.einsum(
        "cmrkz,rzsw->cmskw",
        lax.all_to_all(row_section, "pz", split_axis=3, concat_axis=4, tiled=True),
        z_forward,
        precision=highest,
    )
    vel_spectrum = curl_solve(col_section, y_cells, z_cells)
    z_back = jnp.einsum("cmrkw,rwsz->cmszk", vel_spectrum, z_inverse, precision=highest)
    y_back = jnp.einsum(
        "cmrzk,rksy->czsym",
        lax.all_to_all(z_back, "pz", split_axis=3, concat_axis=4, tiled=True),
        y_inverse,
        precision=highest,
    )
    vel_grid = jnp.einsum(
        "czrym,rmx->czyx",
        lax.all_to_all(y_back, "py", split_axis=3, concat_axis=4, tiled=True),
        x_inverse,
        precision=highest,
    )
    vel_nodes = vel_grid.astype(bf16).astype(f32).reshape(3, node_blocks, BN).transpose(1, 0, 2)
    vel_nodes = jnp.concatenate([vel_nodes, vel_nodes], axis=2)
    return jnp.pad(vel_nodes, ((0, 0), (0, ROWS - 3), (0, 0)))


def per_device(vort_p, pair_weights, pair_part, pair_node, counts):
    n_py, n_pz = lax.axis_size("py"), lax.axis_size("pz")
    node_blocks = NX * CY * CZ // BN
    if (n_py, n_pz) == (N_PY, N_PZ):
        return solve_direct(vort_p, pair_weights, pair_part, pair_node, counts)
    sums, near = spread(vort_p, pair_weights, pair_part, pair_node, counts, node_blocks)
    vel = solve_staged(sums, n_py, n_pz)
    return collect(vel, near, pair_part, pair_node, counts)


def solution(mesh):
    placed = (
        P(None, ("py", "pz")),
        P(("py", "pz"), None, None),
        P(("py", "pz")),
        P(("py", "pz")),
        P(("py", "pz")),
    )
    return jax.shard_map(
        per_device, mesh=mesh, in_specs=placed, out_specs=P(None, ("py", "pz")), check_vma=False
    )
```

```python
import functools
import math

import jax
import jax.numpy as jnp
import numpy as np
from jax import lax
from jax.experimental import pallas as pl
from jax.experimental.pallas import tpu as pltpu
from jax.sharding import PartitionSpec as P

NX = 384
CY = 8
CZ = 2
BP = 128
BN = 64
PB_DEV = 32
ROWS = 8
CHUNK = 32
GROUP = 4
N_PY = 4
N_PZ = 8
MESH = pl.DeviceIdType.MESH
f32 = jnp.float32
bf16 = jnp.bfloat16


def twiddle(row_index, col_index, period):
    product = row_index[:, None] * col_index[None, :] % period
    return product.astype(jnp.float32) * (2.0 * math.pi / period)


def forward_table(length):
    angle = twiddle(jnp.arange(length), jnp.arange(length), length)
    cosine = jnp.cos(angle)
    sines = jnp.sin(angle)
    return jnp.stack([jnp.stack([cosine, -sines], 1), jnp.stack([sines, cosine], 1)], 0)


def inverse_table(length):
    angle = twiddle(jnp.arange(length), jnp.arange(length), length)
    cosine = jnp.cos(angle) / length
    sines = jnp.sin(angle) / length
    return jnp.stack([jnp.stack([cosine, sines], 1), jnp.stack([-sines, cosine], 1)], 0)


def cross_terms(coeffs, field):
    return jnp.stack(
        [
            coeffs[1] * field[2] - coeffs[2] * field[1],
            coeffs[2] * field[0] - coeffs[0] * field[2],
            coeffs[0] * field[1] - coeffs[1] * field[0],
        ],
        axis=0,
    )


def signed_wave(length, index):
    signed = jnp.where(index < length // 2, index, index - length)
    return (signed.astype(jnp.float32) * (2.0 * math.pi / length), index == length // 2)


def curl_solve(spectrum, y_cells, z_cells):
    x_local = spectrum.shape[1]
    y_local = spectrum.shape[3]
    mode_x = lax.axis_index("py") * x_local + jnp.arange(x_local)
    wave_x = mode_x.astype(jnp.float32) * (2.0 * math.pi / NX)
    wave_y, edge_y = signed_wave(y_cells, lax.axis_index("pz") * y_local + jnp.arange(y_local))
    wave_z, edge_z = signed_wave(z_cells, jnp.arange(z_cells))
    wave_x3 = wave_x[:, None, None]
    wave_y3 = wave_y[None, :, None]
    wave_z3 = wave_z[None, None, :]
    total = wave_x3 * wave_x3 + wave_y3 * wave_y3 + wave_z3 * wave_z3
    edges = edge_y[None, :, None] | edge_z[None, None, :]
    keep = (total > 0) & jnp.logical_not(edges)
    inverse_sq = jnp.where(keep, 1.0 / jnp.where(keep, total, 1.0), 0.0)
    inv_wave = (wave_x3 * inverse_sq, wave_y3 * inverse_sq, wave_z3 * inverse_sq)
    real_turn = cross_terms(inv_wave, spectrum[:, :, 0])
    imag_turn = cross_terms(inv_wave, spectrum[:, :, 1])
    return jnp.stack([-imag_turn, real_turn], axis=2)


def halves(table):
    table = np.asarray(table, np.float32)
    high = table.astype(bf16)
    return high, (table - high.astype(np.float32)).astype(bf16)


def split(x):
    high = x.astype(bf16)
    return high, (x - high.astype(f32)).astype(bf16)


def dot(a, b, dims=((1,), (0,))):
    return lax.dot_general(a, b, (dims, ((), ())), preferred_element_type=f32)


def left_half(shape):
    return lax.broadcasted_iota(jnp.int32, shape, 1) < BN


def spread_kernel(part, node, count, parts_ref, w_ref, out_ref, near_ref, parts, sems):
    chunks = w_ref.shape[0] // CHUNK

    def fetch(k):
        here = pl.ds(k * CHUNK, CHUNK)
        return pltpu.make_async_copy(w_ref.at[here], near_ref.at[here], sems.at[k])

    for k in range(chunks):
        fetch(k).start()
    out_ref[...] = jnp.zeros_like(out_ref)
    parts[...] = jnp.zeros_like(parts)
    for b in range(PB_DEV):
        parts[b, 0:3, :] = parts_ref[:, b * BP : (b + 1) * BP].astype(f32)
    left = left_half((ROWS, 128))

    def chunk(k, carry):
        fetch(k).wait()
        base = k * CHUNK
        for g in range(CHUNK // GROUP):
            first = base + g * GROUP
            picked = jnp.concatenate([parts[part[first + i]] for i in range(GROUP)], axis=0)
            tiles = near_ref[pl.ds(first, GROUP)].reshape(GROUP * BN, BP)
            got = dot(picked.astype(bf16), tiles, ((1,), (1,)))
            for i in range(GROUP):
                keep = jnp.logical_and(left if i % 2 == 0 else ~left, first + i < count[0])
                lanes = i // 2 * 128
                own = got[i * ROWS : (i + 1) * ROWS, lanes : lanes + 128]
                out_ref[node[first + i]] += jnp.where(keep, own, 0.0)
        return carry

    lax.fori_loop(0, chunks, chunk, 0)


def spread(vort_p, weights, part, node, counts, node_blocks):
    smem = pl.BlockSpec(memory_space=pltpu.SMEM)
    vmem = pl.BlockSpec(memory_space=pltpu.VMEM)
    return pl.pallas_call(
        spread_kernel,
        out_shape=(
            jax.ShapeDtypeStruct((node_blocks, ROWS, 2 * BN), f32),
            jax.ShapeDtypeStruct(weights.shape, weights.dtype),
        ),
        in_specs=[smem, smem, smem, vmem, pl.BlockSpec(memory_space=pltpu.HBM)],
        out_specs=(vmem, vmem),
        scratch_shapes=[
            pltpu.VMEM((PB_DEV, ROWS, BP), f32),
            pltpu.SemaphoreType.DMA((weights.shape[0] // CHUNK,)),
        ],
        compiler_params=pltpu.CompilerParams(vmem_limit_bytes=48 * 2**20),
        name="spread",
    )(part, node, counts, vort_p, weights)


def collect_kernel(part, node, count, vel_ref, w_ref, out_ref, sums):
    sums[...] = jnp.zeros_like(sums)
    left = left_half((ROWS, 128))
    zero = jnp.zeros((ROWS, 128), f32)

    def chunk(k, carry):
        for g in range(CHUNK // GROUP):
            first = k * CHUNK + g * GROUP
            rows = []
            for i in range(GROUP):
                slot = first + i
                keep = jnp.logical_and(left if i % 2 == 0 else ~left, slot < count[0])
                own = jnp.where(keep, vel_ref[node[slot]], 0.0)
                rows.append(
                    jnp.concatenate(
                        [own if h == i // 2 else zero for h in range(GROUP // 2)], axis=1
                    )
                )
            chosen = jnp.concatenate(rows, axis=0).astype(bf16)
            got = dot(chosen, w_ref[pl.ds(first, GROUP)].reshape(GROUP * BN, BP))
            for i in range(GROUP):
                sums[part[first + i]] += got[i * ROWS : (i + 1) * ROWS]
        return carry

    lax.fori_loop(0, w_ref.shape[0] // CHUNK, chunk, 0)
    for b in range(PB_DEV):
        out_ref[:, b * BP : (b + 1) * BP] = sums[b, 0:3, :]


def collect(vel, weights, part, node, counts):
    smem = pl.BlockSpec(memory_space=pltpu.SMEM)
    vmem = pl.BlockSpec(memory_space=pltpu.VMEM)
    return pl.pallas_call(
        collect_kernel,
        out_shape=jax.ShapeDtypeStruct((3, PB_DEV * BP), f32),
        in_specs=[smem, smem, smem, vmem, vmem],
        out_specs=vmem,
        scratch_shapes=[pltpu.VMEM((PB_DEV, ROWS, BP), f32)],
        compiler_params=pltpu.CompilerParams(vmem_limit_bytes=24 * 2**20),
        name="collect",
    )(part, node, counts, vel, weights)


ORDER = [(2, 6), (3, 6), (3, 7), (2, 7), (2, 3), (1, 7), (1, 6), (2, 2), (3, 2), (3, 4), (3, 5), (3, 3), (2, 5), (2, 4), (1, 5), (1, 4), (0, 7), (1, 3), (2, 1), (0, 6), (1, 2), (3, 1), (3, 0), (2, 0), (1, 0), (0, 3), (1, 1), (0, 4), (0, 5), (0, 2), (0, 1)]


def tables():
    devices = N_PY * N_PZ
    local = NX // 2 // devices
    ny, nz = CY * N_PY, CZ * N_PZ
    row = np.arange(devices * ROWS)
    slot, device = row % ROWS, row // ROWS
    mode = device * local + slot
    angle = 2 * np.pi * (mode[:, None] * np.arange(NX)[None] % NX) / NX
    used = (slot < local)[:, None]
    x_cos, x_sin = np.where(used, np.cos(angle), 0.0), np.where(used, -np.sin(angle), 0.0)
    index = np.arange(devices)
    a, b = index // N_PZ, index % N_PZ
    lane = np.arange(128)
    real, comp, cell = lane // 64, lane % 64 // 16, lane % 16
    zl, yl = cell // CY, cell % CY
    valid = (comp < 3)[None]
    phi = 2 * np.pi * (a[:, None] * yl[None] / ny + b[:, None] * zl[None] / nz)
    sign = np.where(real == 0, 1.0, -1.0)[None]
    turn_cos, turn_sin = np.cos(phi), np.sin(phi) * sign
    psi = 2 * np.pi * (yl[:, None] * yl[None] / CY + zl[:, None] * zl[None] / CZ)
    cosine, sines = np.cos(psi), np.sin(psi)
    r, q = real[:, None], real[None]

    def near(ahead):
        both = np.where(r == q, sines, np.where(r == 0, cosine, -cosine))
        same = (comp[:, None] == (comp[None] + ahead) % 3) & (comp[:, None] < 3) & valid
        return np.where(same, both, 0.0)

    forward = np.concatenate([near(2), near(1)], 1)
    both = np.where(r == q, cosine, np.where(r == 0, sines, -sines))
    same = (comp[:, None] == comp[None]) & (comp[:, None] < 3)
    back = np.where(same, both, 0.0)
    my, mz = a[:, None] + N_PY * yl[None], b[:, None] + N_PZ * zl[None]
    keep = (my != ny // 2) & (mz != nz // 2) & valid
    my, mz = np.where(my < ny // 2, my, my - ny), np.where(mz < nz // 2, mz, mz - nz)
    ky, kz = 2 * np.pi * my / ny, 2 * np.pi * mz / nz
    zero = np.zeros_like(ky)
    wave = np.stack([zero, ky, kz])
    k_first = np.where(comp == 0, wave[1], np.where(comp == 1, wave[2], wave[0]))
    k_second = np.where(comp == 0, wave[2], np.where(comp == 1, wave[0], wave[1]))
    x_first = np.broadcast_to(comp == 2, ky.shape)
    x_second = np.broadcast_to(comp == 1, ky.shape)
    small = [turn_cos, turn_sin, ky * ky + kz * kz, k_first, k_second, x_first, x_second, keep]
    small = np.stack(small).astype(np.float32)
    near_table = np.concatenate([forward, back], 1)
    near_high = near_table.astype(np.float32).astype(bf16)
    return [
        *halves(np.concatenate([x_cos, x_sin], 1)),
        np.concatenate([near_high, near_high], 0),
        small,
    ]


def flip(index, bits):
    for bit in (1, 2, 4):
        if bits & bit:
            index = index + bit - 2 * bit * (index // bit % 2)
    return index


def swap(x):
    return pltpu.roll(x, 64, 1)


def line_transform(x, turn):
    if len(x) == 2:
        return [x[0] + x[1], x[0] - x[1]]
    half = len(x) // 2
    even = [x[k] + x[k + half] for k in range(half)]
    odd = [x[k] - x[k + half] for k in range(half)]
    if half == 2:
        side = turn(odd[1])
        low, high = line_transform(even, turn), [odd[0] + side, odd[0] - side]
    else:
        side = turn(odd[2])
        near, far = odd[1] - odd[3], turn(odd[1] + odd[3])
        root = math.sqrt(0.5)
        plus, minus = (near + far) * root, (far - near) * root
        first, second = odd[0] + side, odd[0] - side
        low = line_transform(even, turn)
        high = [first + plus, second + minus, first - plus, second - minus]
    return [value for pair in zip(low, high) for value in pair]


def plane_transform(blocks, turn):
    columns = [
        line_transform([blocks[a * N_PZ + b] for a in range(N_PY)], turn) for b in range(N_PZ)
    ]
    lines = [line_transform([columns[b][a] for b in range(N_PZ)], turn) for a in range(N_PY)]
    return [lines[a][b] for a in range(N_PY) for b in range(N_PZ)]


def solve_kernel(
    count,
    part_hbm,
    node_hbm,
    parts_hbm,
    w_ref,
    xh_hbm,
    xl_hbm,
    near_hbm,
    small_hbm,
    near_ref,
    vel_ref,
    choose_ref,
    gather_ref,
    part_ref,
    node_ref,
    parts_ref,
    xh_ref,
    xl_ref,
    tab_ref,
    small,
    send_a,
    recv_a,
    send_b,
    recv_b,
    send_sem,
    recv_sem,
    parts,
    picks,
    pairs,
    held,
    sems,
    const_sems,
    first_sems,
):
    devices = N_PY * N_PZ
    local = NX // 2 // devices
    rows = devices * ROWS
    per_row = NX // BN
    cells = CY * CZ
    groups = w_ref.shape[1]
    slots = GROUP * groups
    chunks = sems.shape[0]
    step = groups // chunks
    my_y, my_z = lax.axis_index("py"), lax.axis_index("pz")
    me = my_y * N_PZ + my_z
    others = [(flip(my_y, ky), flip(my_z, kz)) for ky, kz in ORDER]

    def fetch(k):
        here = pl.ds(k * step, step)
        return pltpu.make_async_copy(w_ref.at[:, here], near_ref.at[:, here], sems.at[k])

    firsts = [
        pltpu.make_async_copy(c, h, first_sems.at[i])
        for i, (c, h) in enumerate(
            ((parts_hbm, parts_ref), (part_hbm, part_ref), (node_hbm, node_ref))
        )
    ]
    for load in firsts:
        load.start()
    for k in range(chunks):
        fetch(k).start()
    if not False:
        barrier = pltpu.get_barrier_semaphore()
        for other in others:
            pl.semaphore_signal(barrier, inc=1, device_id=other, device_id_type=MESH)
    loads = [
        pltpu.make_async_copy(c, h, const_sems.at[i])
        for i, (c, h) in enumerate(
            ((xh_hbm, xh_ref), (xl_hbm, xl_ref), (near_hbm, tab_ref), (small_hbm, small))
        )
    ]
    for load in loads:
        load.start()

    sent = pl.ds(0, local)

    def exchange(send, recv, phase):
        if False:
            recv[...] = send[...]
            return
        for to_y, to_z in others:
            pltpu.make_async_remote_copy(
                src_ref=send.at[to_y * N_PZ + to_z, sent],
                dst_ref=recv.at[me, sent],
                send_sem=send_sem.at[phase],
                recv_sem=recv_sem.at[phase],
                device_id=(to_y, to_z),
                device_id_type=MESH,
            ).start()

    def wait_all(buffer, sem):
        if False:
            return
        many = pl.ds(0, devices - 1)
        pltpu.make_async_copy(buffer.at[many, sent], buffer.at[many, sent], sem).wait()

    def stop(value):
        vel_ref[...] = jnp.zeros_like(vel_ref) + value.astype(bf16)
        choose_ref[...] = jnp.zeros_like(choose_ref)
        gather_ref[...] = jnp.zeros_like(gather_ref)

    def wait_fetches():
        for k in range(chunks):
            fetch(k).wait()
        for load in loads:
            load.wait()

    for load in firsts:
        load.wait()
    if 0 == 1:
        wait_fetches()
        return stop(jnp.zeros((1, 128), f32))

    for b in range(PB_DEV):
        parts[b * ROWS : b * ROWS + 3, :] = parts_ref[:, b * BP : (b + 1) * BP].astype(f32)
    row = lax.broadcasted_iota(jnp.int32, (PB_DEV, slots), 0)
    chooser = jnp.where(row == part_ref[...], 1.0, 0.0).T.astype(bf16)
    tall = GROUP * 4
    for c in range(3):
        block = parts[pl.ds(c, PB_DEV, stride=ROWS), :].astype(bf16)
        got = dot(chooser, block)
        for i in range(GROUP):
            here = pl.ds(c * GROUP + i, groups, stride=tall)
            picks[here, :] = got[i * groups : (i + 1) * groups]
    if 0 == 2:
        wait_fetches()
        return stop(picks[0:1])
    if 0 == 3:
        wait_fetches()
    sub = lax.broadcasted_iota(jnp.int32, (tall, 128), 0) % GROUP
    half = lax.broadcasted_iota(jnp.int32, (tall, 128), 1) // BN
    low_slots = sub < 2
    own_half = sub % 2 == half
    for k in range(chunks):
        if 0 != 3:
            fetch(k).wait()
        for g in range(k * step, (k + 1) * step):
            picked = picks[g * tall : (g + 1) * tall, :].astype(bf16)
            tiles = near_ref[:, g].reshape(GROUP * BN, BP)
            got = dot(picked, tiles, ((1,), (1,)))
            own = jnp.where(low_slots, got[:, :128], got[:, 128:])
            pairs[g * tall : (g + 1) * tall, :] = jnp.where(own_half, own, 0.0)
    if 0 != 3:
        for load in loads:
            load.wait()
    if 0 == 3 or 0 == 4:
        return stop(pairs[0:1])

    def pairs_of(c):
        return jnp.concatenate(
            [pairs[pl.ds(c * GROUP + i, groups, stride=tall), :] for i in range(GROUP)], axis=0
        )

    row = lax.broadcasted_iota(jnp.int32, (cells * per_row, slots), 0)
    block = row % cells * per_row + row // cells
    live = lax.broadcasted_iota(jnp.int32, (cells * per_row, slots), 1) < count[0]
    hits = jnp.where((block == node_ref[...]) & live, 1.0, 0.0)
    choose_ref[...] = hits.T.astype(bf16)
    hits = hits.astype(bf16)
    left = left_half((cells, 128))
    lines = []
    for c in range(3):
        total = dot(hits, jnp.concatenate(split(pairs_of(c)), axis=1))
        total = total[:, :128] + total[:, 128:]
        total += swap(total)
        pieces = [
            jnp.where(
                left, total[xb * cells : (xb + 1) * cells], total[(xb + 1) * cells : (xb + 2) * cells]
            )
            for xb in range(0, per_row, 2)
        ]
        lines.append(jnp.concatenate(pieces, axis=1))
    vort = jnp.concatenate([*lines, jnp.zeros((cells, NX), f32)], axis=0)
    if 0 == 5:
        return stop(vort[0:1, 0:128])
    high, rest = split(vort)
    none = jnp.zeros_like(high)
    both = [
        jnp.concatenate(
            [jnp.concatenate([x, none], axis=1), jnp.concatenate([none, x], axis=1)], axis=0
        )
        for x in (high, rest)
    ]
    over = ((1,), (1,))
    modes = dot(xh_ref[...], jnp.concatenate(both, axis=0), over)
    modes = modes[:, :128] + (modes[:, 128:] + dot(xl_ref[...], both[0], over))
    send_a[...] = modes.reshape(devices, ROWS, 128)
    recv_a[me] = send_a[me]
    if 0 == 6:
        return stop(send_a[0, 0:1])
    if not False:
        pl.semaphore_wait(barrier, devices - 1)
    exchange(send_a, recv_a, 0)

    unsent = jnp.zeros((devices, ROWS - local, 128), f32)
    recv_b[:, local:, :] = unsent
    row = lax.broadcasted_iota(jnp.int32, (PB_DEV, slots), 0)
    live = lax.broadcasted_iota(jnp.int32, (PB_DEV, slots), 1) < count[0]
    gather_ref[...] = jnp.where((row == part_ref[...]) & live, 1.0, 0.0).astype(bf16)

    def spread_out(i):
        return jnp.broadcast_to(small[i][:, None, :], (devices, ROWS, 128)).reshape(rows, 128)

    slot = lax.broadcasted_iota(jnp.int32, (rows, 128), 0) % ROWS
    mode = me * local + slot
    wave_x = mode.astype(f32) * (2.0 * math.pi / NX)
    total = spread_out(2) + wave_x * wave_x
    weight = jnp.where(mode == 0, 1.0, 2.0) * (1.0 / (NX * CY * N_PY * CZ * N_PZ))
    inverse = spread_out(7) * weight / jnp.where(total > 0, total, 1.0)
    held[0] = (spread_out(3) + wave_x * spread_out(5)) * inverse
    held[1] = (spread_out(4) + wave_x * spread_out(6)) * inverse
    held[2], held[3] = spread_out(0), spread_out(1)
    sign = jnp.where(lax.broadcasted_iota(jnp.int32, (ROWS, 128), 1) < 64, 1.0, -1.0)

    def ahead(x):
        return swap(x) * sign

    def astern(x):
        return swap(x) * -sign

    def along(x, table):
        return dot(jnp.concatenate(split(x), axis=1), table)

    wait_all(recv_a, recv_sem.at[0])
    if 0 == 7:
        return stop(recv_a[0, 0:1] + held[0, 0:1] + held[1, 0:1] + held[2, 0:1] + held[3, 0:1])
    y = plane_transform([recv_a[d] for d in range(devices)], ahead)
    y = jnp.concatenate(y, axis=0)
    if 0 == 8:
        send_b[...] = y.reshape(devices, ROWS, 128)
        return stop(send_b[0, 0:1])
    z = held[2] * y + held[3] * swap(y)
    both = along(z, tab_ref[:, 0:256])
    if 0 == 9:
        send_b[...] = (both[:, :128] + both[:, 128:]).reshape(devices, ROWS, 128)
        return stop(send_b[0, 0:1])
    vel = held[0] * both[:, :128] - held[1] * both[:, 128:]
    y = along(vel, tab_ref[:, 256:384])
    z = held[2] * y - held[3] * swap(y)
    if 0 == 10:
        send_b[...] = z.reshape(devices, ROWS, 128)
        return stop(send_b[0, 0:1])
    z = plane_transform([z[d * ROWS : (d + 1) * ROWS] for d in range(devices)], astern)
    for d in range(devices):
        send_b[d] = z[d]
    recv_b[me, 0:local] = send_b[me, 0:local]
    if 0 == 11:
        return stop(send_b[0, 0:1])
    exchange(send_b, recv_b, 1)
    wait_all(send_a, send_sem.at[0])
    wait_all(recv_b, recv_sem.at[1])
    back = recv_b[...].reshape(rows, 128).T
    grid = jnp.zeros((48, NX), f32)
    for k in range(2):
        high, rest = split(back[64 * k : 64 * k + 48])
        table = xh_ref[:, k * NX : (k + 1) * NX]
        both = dot(jnp.concatenate([high, rest], axis=0), table)
        grid += both[:48] + (both[48:] + dot(high, xl_ref[:, k * NX : (k + 1) * NX]))
    if 0 == 12:
        return stop(grid[0:1, 0:128])
    for c in range(3):
        for xb in range(0, per_row, 2):
            piece = grid[c * cells : (c + 1) * cells, xb * BN : (xb + 2) * BN]
            other = swap(piece)
            for h, line in ((0, jnp.where(left, piece, other)), (1, jnp.where(left, other, piece))):
                vel_ref[c, (xb + h) * cells : (xb + h + 1) * cells, :] = line.astype(bf16)
    wait_all(send_b, send_sem.at[1])


def collect_kernel_b(vel_ref, choose_ref, gather_ref, w_ref, out_ref, picks, pairs, sums):
    groups = w_ref.shape[1]
    tall = GROUP * 4
    picks[...] = jnp.zeros_like(picks)
    chooser = choose_ref[...]
    for c in range(3):
        got = dot(chooser, vel_ref[c])
        for i in range(GROUP):
            here = pl.ds(c * GROUP + i, groups, stride=tall)
            picks[here, :] = got[i * groups : (i + 1) * groups]
    sub = lax.broadcasted_iota(jnp.int32, (tall, 128), 0) % GROUP
    half = lax.broadcasted_iota(jnp.int32, (tall, 128), 1) // BN
    first = (sub < 2) & (sub % 2 == half)
    second = (sub >= 2) & (sub % 2 == half)
    for g in range(groups):
        line = picks[g * tall : (g + 1) * tall, :]
        chosen = jnp.concatenate([jnp.where(first, line, 0.0), jnp.where(second, line, 0.0)], axis=1)
        pairs[g * tall : (g + 1) * tall, :] = dot(
            chosen.astype(bf16), w_ref[:, g].reshape(GROUP * BN, BP)
        )
    for c in range(3):
        lines = jnp.concatenate(
            [pairs[pl.ds(c * GROUP + i, groups, stride=tall), :] for i in range(GROUP)], axis=0
        )
        total = dot(gather_ref[...], jnp.concatenate(split(lines), axis=1))
        sums[pl.ds(c, PB_DEV, stride=ROWS), :] = total[:, :128] + total[:, 128:]
    for b in range(PB_DEV):
        out_ref[:, b * BP : (b + 1) * BP] = sums[b * ROWS : b * ROWS + 3, :]


def solve_direct(vort_p, weights, part, node, counts):
    devices = N_PY * N_PZ
    node_blocks = NX * CY * CZ // BN
    slots = weights.shape[0]
    groups = slots // GROUP
    vmem = pl.BlockSpec(memory_space=pltpu.VMEM)
    hbm = pl.BlockSpec(memory_space=pltpu.HBM)
    block = pltpu.VMEM((devices, ROWS, 128), f32)
    consts = [jnp.asarray(t) for t in tables()]
    weights = weights.reshape(GROUP, groups, BN, BP)
    inputs = [part[None], node[None], vort_p, weights, *consts]
    tall = pltpu.VMEM((groups * GROUP * 4, 128), f32)
    near, vel, chooser, gather = pl.pallas_call(
        solve_kernel,
        out_shape=(
            jax.ShapeDtypeStruct(weights.shape, weights.dtype),
            jax.ShapeDtypeStruct((3, node_blocks, 128), bf16),
            jax.ShapeDtypeStruct((slots, node_blocks), bf16),
            jax.ShapeDtypeStruct((PB_DEV, slots), bf16),
        ),
        in_specs=[pl.BlockSpec(memory_space=pltpu.SMEM)] + [hbm] * len(inputs),
        out_specs=(vmem, vmem, vmem, vmem),
        scratch_shapes=[
            pltpu.VMEM((1, slots), jnp.int32),
            pltpu.VMEM((1, slots), jnp.int32),
            pltpu.VMEM(vort_p.shape, vort_p.dtype),
            *[pltpu.VMEM(t.shape, t.dtype) for t in consts],
            block,
            block,
            block,
            block,
            pltpu.SemaphoreType.DMA((2,)),
            pltpu.SemaphoreType.DMA((2,)),
            pltpu.VMEM((PB_DEV * ROWS, BP), f32),
            tall,
            tall,
            pltpu.VMEM((4, devices * ROWS, 128), f32),
            pltpu.SemaphoreType.DMA((2,)),
            pltpu.SemaphoreType.DMA((len(consts),)),
            pltpu.SemaphoreType.DMA((3,)),
        ],
        compiler_params=pltpu.CompilerParams(
            collective_id=None if False else 0, has_side_effects=True, vmem_limit_bytes=24 * 2**20
        ),
        name="solve",
    )(counts, *[pltpu.with_memory_space_constraint(x, pltpu.HBM) for x in inputs])
    return pl.pallas_call(
        collect_kernel_b,
        out_shape=jax.ShapeDtypeStruct((3, PB_DEV * BP), f32),
        in_specs=[vmem] * 4,
        out_specs=vmem,
        scratch_shapes=[tall, tall, pltpu.VMEM((PB_DEV * ROWS, BP), f32)],
        compiler_params=pltpu.CompilerParams(vmem_limit_bytes=16 * 2**20),
        name="collect_last",
    )(vel, chooser, gather, near)


def solve_staged(sums, n_py, n_pz):
    highest = lax.Precision.HIGHEST
    node_blocks = sums.shape[0]
    y_cells, z_cells = CY * n_py, CZ * n_pz
    x_modes = NX // 2
    sums = sums[:, :3, :BN] + sums[:, :3, BN:]
    vort_grid = sums.transpose(1, 0, 2).reshape(3, CZ, CY, NX)
    angle_fwd = twiddle(jnp.arange(NX), jnp.arange(x_modes), NX)
    x_forward = jnp.stack([jnp.cos(angle_fwd), -jnp.sin(angle_fwd)], 1)
    angle_inv = twiddle(jnp.arange(x_modes), jnp.arange(NX), NX)
    mode_weight = (jnp.where(jnp.arange(x_modes) == 0, 1.0, 2.0) / NX)[:, None]
    x_inverse = jnp.stack([mode_weight * jnp.cos(angle_inv), -mode_weight * jnp.sin(angle_inv)], 0)
    y_forward = forward_table(y_cells)
    z_forward = forward_table(z_cells)
    z_inverse = inverse_table(z_cells)
    y_inverse = inverse_table(y_cells)
    x_spectrum = jnp.einsum("czyx,xrm->czrmy", vort_grid, x_forward, precision=highest)
    row_section = jnp.einsum(
        "czrmy,rysk->cmskz",
        lax.all_to_all(x_spectrum, "py", split_axis=3, concat_axis=4, tiled=True),
        y_forward,
        precision=highest,
    )
    col_section = jnp.einsum(
        "cmrkz,rzsw->cmskw",
        lax.all_to_all(row_section, "pz", split_axis=3, concat_axis=4, tiled=True),
        z_forward,
        precision=highest,
    )
    vel_spectrum = curl_solve(col_section, y_cells, z_cells)
    z_back = jnp.einsum("cmrkw,rwsz->cmszk", vel_spectrum, z_inverse, precision=highest)
    y_back = jnp.einsum(
        "cmrzk,rksy->czsym",
        lax.all_to_all(z_back, "pz", split_axis=3, concat_axis=4, tiled=True),
        y_inverse,
        precision=highest,
    )
    vel_grid = jnp.einsum(
        "czrym,rmx->czyx",
        lax.all_to_all(y_back, "py", split_axis=3, concat_axis=4, tiled=True),
        x_inverse,
        precision=highest,
    )
    vel_nodes = vel_grid.astype(bf16).astype(f32).reshape(3, node_blocks, BN).transpose(1, 0, 2)
    vel_nodes = jnp.concatenate([vel_nodes, vel_nodes], axis=2)
    return jnp.pad(vel_nodes, ((0, 0), (0, ROWS - 3), (0, 0)))


def per_device(vort_p, pair_weights, pair_part, pair_node, counts):
    n_py, n_pz = lax.axis_size("py"), lax.axis_size("pz")
    node_blocks = NX * CY * CZ // BN
    if (n_py, n_pz) == (N_PY, N_PZ):
        return solve_direct(vort_p, pair_weights, pair_part, pair_node, counts)
    sums, near = spread(vort_p, pair_weights, pair_part, pair_node, counts, node_blocks)
    vel = solve_staged(sums, n_py, n_pz)
    return collect(vel, near, pair_part, pair_node, counts)


def solution(mesh):
    placed = (
        P(None, ("py", "pz")),
        P(("py", "pz"), None, None),
        P(("py", "pz")),
        P(("py", "pz")),
        P(("py", "pz")),
    )
    return jax.shard_map(
        per_device, mesh=mesh, in_specs=placed, out_specs=P(None, ("py", "pz")), check_vma=False
    )
```

```python
import functools
import math

import jax
import jax.numpy as jnp
import numpy as np
from jax import lax
from jax.experimental import pallas as pl
from jax.experimental.pallas import tpu as pltpu
from jax.sharding import PartitionSpec as P

NX = 384
CY = 8
CZ = 2
BP = 128
BN = 64
PB_DEV = 32
ROWS = 8
CHUNK = 32
GROUP = 4
N_PY = 4
N_PZ = 8
MESH = pl.DeviceIdType.MESH
f32 = jnp.float32
bf16 = jnp.bfloat16


def twiddle(row_index, col_index, period):
    product = row_index[:, None] * col_index[None, :] % period
    return product.astype(jnp.float32) * (2.0 * math.pi / period)


def forward_table(length):
    angle = twiddle(jnp.arange(length), jnp.arange(length), length)
    cosine = jnp.cos(angle)
    sines = jnp.sin(angle)
    return jnp.stack([jnp.stack([cosine, -sines], 1), jnp.stack([sines, cosine], 1)], 0)


def inverse_table(length):
    angle = twiddle(jnp.arange(length), jnp.arange(length), length)
    cosine = jnp.cos(angle) / length
    sines = jnp.sin(angle) / length
    return jnp.stack([jnp.stack([cosine, sines], 1), jnp.stack([-sines, cosine], 1)], 0)


def cross_terms(coeffs, field):
    return jnp.stack(
        [
            coeffs[1] * field[2] - coeffs[2] * field[1],
            coeffs[2] * field[0] - coeffs[0] * field[2],
            coeffs[0] * field[1] - coeffs[1] * field[0],
        ],
        axis=0,
    )


def signed_wave(length, index):
    signed = jnp.where(index < length // 2, index, index - length)
    return (signed.astype(jnp.float32) * (2.0 * math.pi / length), index == length // 2)


def curl_solve(spectrum, y_cells, z_cells):
    x_local = spectrum.shape[1]
    y_local = spectrum.shape[3]
    mode_x = lax.axis_index("py") * x_local + jnp.arange(x_local)
    wave_x = mode_x.astype(jnp.float32) * (2.0 * math.pi / NX)
    wave_y, edge_y = signed_wave(y_cells, lax.axis_index("pz") * y_local + jnp.arange(y_local))
    wave_z, edge_z = signed_wave(z_cells, jnp.arange(z_cells))
    wave_x3 = wave_x[:, None, None]
    wave_y3 = wave_y[None, :, None]
    wave_z3 = wave_z[None, None, :]
    total = wave_x3 * wave_x3 + wave_y3 * wave_y3 + wave_z3 * wave_z3
    edges = edge_y[None, :, None] | edge_z[None, None, :]
    keep = (total > 0) & jnp.logical_not(edges)
    inverse_sq = jnp.where(keep, 1.0 / jnp.where(keep, total, 1.0), 0.0)
    inv_wave = (wave_x3 * inverse_sq, wave_y3 * inverse_sq, wave_z3 * inverse_sq)
    real_turn = cross_terms(inv_wave, spectrum[:, :, 0])
    imag_turn = cross_terms(inv_wave, spectrum[:, :, 1])
    return jnp.stack([-imag_turn, real_turn], axis=2)


def halves(table):
    table = np.asarray(table, np.float32)
    high = table.astype(bf16)
    return high, (table - high.astype(np.float32)).astype(bf16)


def split(x):
    high = x.astype(bf16)
    return high, (x - high.astype(f32)).astype(bf16)


def dot(a, b, dims=((1,), (0,))):
    return lax.dot_general(a, b, (dims, ((), ())), preferred_element_type=f32)


def left_half(shape):
    return lax.broadcasted_iota(jnp.int32, shape, 1) < BN


def spread_kernel(part, node, count, parts_ref, w_ref, out_ref, near_ref, parts, sems):
    chunks = w_ref.shape[0] // CHUNK

    def fetch(k):
        here = pl.ds(k * CHUNK, CHUNK)
        return pltpu.make_async_copy(w_ref.at[here], near_ref.at[here], sems.at[k])

    for k in range(chunks):
        fetch(k).start()
    out_ref[...] = jnp.zeros_like(out_ref)
    parts[...] = jnp.zeros_like(parts)
    for b in range(PB_DEV):
        parts[b, 0:3, :] = parts_ref[:, b * BP : (b + 1) * BP].astype(f32)
    left = left_half((ROWS, 128))

    def chunk(k, carry):
        fetch(k).wait()
        base = k * CHUNK
        for g in range(CHUNK // GROUP):
            first = base + g * GROUP
            picked = jnp.concatenate([parts[part[first + i]] for i in range(GROUP)], axis=0)
            tiles = near_ref[pl.ds(first, GROUP)].reshape(GROUP * BN, BP)
            got = dot(picked.astype(bf16), tiles, ((1,), (1,)))
            for i in range(GROUP):
                keep = jnp.logical_and(left if i % 2 == 0 else ~left, first + i < count[0])
                lanes = i // 2 * 128
                own = got[i * ROWS : (i + 1) * ROWS, lanes : lanes + 128]
                out_ref[node[first + i]] += jnp.where(keep, own, 0.0)
        return carry

    lax.fori_loop(0, chunks, chunk, 0)


def spread(vort_p, weights, part, node, counts, node_blocks):
    smem = pl.BlockSpec(memory_space=pltpu.SMEM)
    vmem = pl.BlockSpec(memory_space=pltpu.VMEM)
    return pl.pallas_call(
        spread_kernel,
        out_shape=(
            jax.ShapeDtypeStruct((node_blocks, ROWS, 2 * BN), f32),
            jax.ShapeDtypeStruct(weights.shape, weights.dtype),
        ),
        in_specs=[smem, smem, smem, vmem, pl.BlockSpec(memory_space=pltpu.HBM)],
        out_specs=(vmem, vmem),
        scratch_shapes=[
            pltpu.VMEM((PB_DEV, ROWS, BP), f32),
            pltpu.SemaphoreType.DMA((weights.shape[0] // CHUNK,)),
        ],
        compiler_params=pltpu.CompilerParams(vmem_limit_bytes=48 * 2**20),
        name="spread",
    )(part, node, counts, vort_p, weights)


def collect_kernel(part, node, count, vel_ref, w_ref, out_ref, sums):
    sums[...] = jnp.zeros_like(sums)
    left = left_half((ROWS, 128))
    zero = jnp.zeros((ROWS, 128), f32)

    def chunk(k, carry):
        for g in range(CHUNK // GROUP):
            first = k * CHUNK + g * GROUP
            rows = []
            for i in range(GROUP):
                slot = first + i
                keep = jnp.logical_and(left if i % 2 == 0 else ~left, slot < count[0])
                own = jnp.where(keep, vel_ref[node[slot]], 0.0)
                rows.append(
                    jnp.concatenate(
                        [own if h == i // 2 else zero for h in range(GROUP // 2)], axis=1
                    )
                )
            chosen = jnp.concatenate(rows, axis=0).astype(bf16)
            got = dot(chosen, w_ref[pl.ds(first, GROUP)].reshape(GROUP * BN, BP))
            for i in range(GROUP):
                sums[part[first + i]] += got[i * ROWS : (i + 1) * ROWS]
        return carry

    lax.fori_loop(0, w_ref.shape[0] // CHUNK, chunk, 0)
    for b in range(PB_DEV):
        out_ref[:, b * BP : (b + 1) * BP] = sums[b, 0:3, :]


def collect(vel, weights, part, node, counts):
    smem = pl.BlockSpec(memory_space=pltpu.SMEM)
    vmem = pl.BlockSpec(memory_space=pltpu.VMEM)
    return pl.pallas_call(
        collect_kernel,
        out_shape=jax.ShapeDtypeStruct((3, PB_DEV * BP), f32),
        in_specs=[smem, smem, smem, vmem, vmem],
        out_specs=vmem,
        scratch_shapes=[pltpu.VMEM((PB_DEV, ROWS, BP), f32)],
        compiler_params=pltpu.CompilerParams(vmem_limit_bytes=24 * 2**20),
        name="collect",
    )(part, node, counts, vel, weights)


EDGES = (0, 28, 64)
MIDS = 2 * N_PZ
TALL = 16
PARTNERS = (6, 7, 4, 5, 2, 3, 1, 0)
HOPS = {0: 0, 1: 0, 2: 1, 3: 1, 4: 1, 5: 1, 6: 2, 7: 2}


def by_hops(planes):
    pairs = [(plane, kz) for plane in range(len(planes)) for kz in PARTNERS]
    return sorted(pairs, key=lambda pair: -(planes[pair[0]] + HOPS[pair[1]]))


def tables():
    devices = N_PY * N_PZ
    local = NX // 2 // MIDS
    ny, nz = CY * N_PY, CZ * N_PZ
    row = np.arange(MIDS * TALL)
    slot, device = row % TALL, row // TALL
    mode = device * local + slot
    angle = 2 * np.pi * (mode[:, None] * np.arange(NX)[None] % NX) / NX
    used = (slot < local)[:, None]
    x_cos, x_sin = np.where(used, np.cos(angle), 0.0), np.where(used, -np.sin(angle), 0.0)
    index = np.arange(devices)
    a, b = index // N_PZ, index % N_PZ
    lane = np.arange(128)
    real, comp, cell = lane // 64, lane % 64 // 16, lane % 16
    zl, yl = cell // CY, cell % CY
    valid = (comp < 3)[None]
    phi = 2 * np.pi * (a[:, None] * yl[None] / ny + b[:, None] * zl[None] / nz)
    sign = np.where(real == 0, 1.0, -1.0)[None]
    turn_cos, turn_sin = np.cos(phi), np.sin(phi) * sign
    psi = 2 * np.pi * (yl[:, None] * yl[None] / CY + zl[:, None] * zl[None] / CZ)
    cosine, sines = np.cos(psi), np.sin(psi)
    r, q = real[:, None], real[None]

    def near(ahead):
        both = np.where(r == q, sines, np.where(r == 0, cosine, -cosine))
        same = (comp[:, None] == (comp[None] + ahead) % 3) & (comp[:, None] < 3) & valid
        return np.where(same, both, 0.0)

    forward = np.concatenate([near(2), near(1)], 1)
    both = np.where(r == q, cosine, np.where(r == 0, sines, -sines))
    same = (comp[:, None] == comp[None]) & (comp[:, None] < 3)
    back = np.where(same, both, 0.0)
    my, mz = a[:, None] + N_PY * yl[None], b[:, None] + N_PZ * zl[None]
    keep = (my != ny // 2) & (mz != nz // 2) & valid
    my, mz = np.where(my < ny // 2, my, my - ny), np.where(mz < nz // 2, mz, mz - nz)
    ky, kz = 2 * np.pi * my / ny, 2 * np.pi * mz / nz
    zero = np.zeros_like(ky)
    wave = np.stack([zero, ky, kz])
    k_first = np.where(comp == 0, wave[1], np.where(comp == 1, wave[2], wave[0]))
    k_second = np.where(comp == 0, wave[2], np.where(comp == 1, wave[0], wave[1]))
    x_first = np.broadcast_to(comp == 2, ky.shape)
    x_second = np.broadcast_to(comp == 1, ky.shape)
    small = [turn_cos, turn_sin, ky * ky + kz * kz, k_first, k_second, x_first, x_second, keep]
    small = np.stack(small).astype(np.float32)
    near_table = np.concatenate([forward, back], 1)
    near_high = near_table.astype(np.float32).astype(bf16)
    return [
        np.concatenate(halves(np.concatenate([x_cos, x_sin], 1)), 1),
        np.concatenate([near_high, near_high], 0),
        small,
    ]


def flip(index, bits):
    for bit in (1, 2, 4):
        if bits & bit:
            index = index + bit - 2 * bit * (index // bit % 2)
    return index


def swap(x):
    return pltpu.roll(x, 64, 1)


def line_transform(x, turn):
    if len(x) == 2:
        return [x[0] + x[1], x[0] - x[1]]
    half = len(x) // 2
    even = [x[k] + x[k + half] for k in range(half)]
    odd = [x[k] - x[k + half] for k in range(half)]
    if half == 2:
        side = turn(odd[1])
        low, high = line_transform(even, turn), [odd[0] + side, odd[0] - side]
    else:
        side = turn(odd[2])
        near, far = odd[1] - odd[3], turn(odd[1] + odd[3])
        root = math.sqrt(0.5)
        plus, minus = (near + far) * root, (far - near) * root
        first, second = odd[0] + side, odd[0] - side
        low = line_transform(even, turn)
        high = [first + plus, second + minus, first - plus, second - minus]
    return [value for pair in zip(low, high) for value in pair]


def solve_kernel(
    count,
    part_hbm,
    node_hbm,
    parts_hbm,
    w_ref,
    x_hbm,
    near_hbm,
    small_hbm,
    near_ref,
    vel_ref,
    choose_ref,
    gather_ref,
    part_ref,
    node_ref,
    parts_ref,
    x_ref,
    tab_ref,
    small,
    send_a,
    recv_a,
    send_b,
    recv_b,
    send_sem,
    recv_sem,
    parts,
    picks,
    pairs,
    held,
    sems,
    const_sems,
    first_sems,
    plane_sem,
):
    devices = N_PY * N_PZ
    local = NX // 2 // MIDS
    rows = devices * TALL
    per_row = NX // BN
    cells = CY * CZ
    groups = w_ref.shape[1]
    slots = GROUP * groups
    chunks = sems.shape[0]
    my_y, my_z = lax.axis_index("py"), lax.axis_index("pz")
    me = my_y * N_PZ + my_z
    mid = (my_y == 1) | (my_y == 2)
    outer = jnp.logical_not(mid)
    my_mid = me - N_PZ
    near_plane, far_plane = 1 + my_y // 2, 2 - my_y // 2
    opposite = 6 - 3 * my_y
    mid_planes = (opposite, 3 - opposite, 3 - my_y, my_y)
    to_mids = [((far_plane, near_plane)[p], flip(my_z, kz)) for p, kz in by_hops((2, 1))]
    order = [pair for pair in by_hops((2, 1, 1, 0)) if pair != (3, 0)]
    to_all = [(mid_planes[p], flip(my_z, kz)) for p, kz in order]

    def fetch(k):
        here = pl.ds(EDGES[k], EDGES[k + 1] - EDGES[k])
        return pltpu.make_async_copy(w_ref.at[:, here], near_ref.at[:, here], sems.at[k])

    firsts = [
        pltpu.make_async_copy(c, h, first_sems.at[i])
        for i, (c, h) in enumerate(
            ((parts_hbm, parts_ref), (part_hbm, part_ref), (node_hbm, node_ref))
        )
    ]
    for load in firsts:
        load.start()
    for k in range(chunks):
        fetch(k).start()
    if not False:
        barrier = pltpu.get_barrier_semaphore()

        @pl.when(mid)
        def _():
            for other in to_all:
                pl.semaphore_signal(barrier, inc=1, device_id=other, device_id_type=MESH)

        @pl.when(outer)
        def _():
            for other in to_mids:
                pl.semaphore_signal(barrier, inc=1, device_id=other, device_id_type=MESH)

    loads = [
        pltpu.make_async_copy(c, h, const_sems.at[i])
        for i, (c, h) in enumerate(
            ((x_hbm, x_ref), (near_hbm, tab_ref), (small_hbm, small))
        )
    ]

    packed = 3 * local // 4
    sent = pl.ds(0, packed)
    spare = lax.broadcasted_iota(jnp.int32, (1, 128), 1) % 64 // 16

    def pack(buffer, first, many):
        lines = buffer.reshape(buffer.shape[0] * TALL, 128)
        for j in range(local - packed):
            extra = lines[pl.ds(first * TALL + packed + j, many, stride=TALL), :]
            for c in range(3):
                here = pl.ds(first * TALL + 3 * j + c, many, stride=TALL)
                moved = pltpu.roll(extra, 16 * (3 - c), 1)
                lines[here, :] = jnp.where(spare == 3, moved, lines[here, :])

    def unpack(buffer, first, many):
        lines = buffer.reshape(buffer.shape[0] * TALL, 128)
        for j in range(local - packed):
            extra = jnp.zeros((many, 128), f32)
            for c in range(3):
                line = lines[pl.ds(first * TALL + 3 * j + c, many, stride=TALL), :]
                moved = pltpu.roll(line, 128 - 16 * (3 - c), 1)
                extra = jnp.where(spare == c, moved, extra)
            lines[pl.ds(first * TALL + packed + j, many, stride=TALL), :] = extra

    def push(source, target, phase, landed, device):
        pltpu.make_async_remote_copy(
            src_ref=source.at[sent],
            dst_ref=target.at[sent],
            send_sem=send_sem.at[phase],
            recv_sem=landed,
            device_id=device,
            device_id_type=MESH,
        ).start()

    def wait_blocks(buffer, many, sem):
        blocks = buffer.at[pl.ds(0, many), sent]
        pltpu.make_async_copy(blocks, blocks, sem).wait()

    def stop(value):
        vel_ref[...] = jnp.zeros_like(vel_ref) + value.astype(bf16)
        choose_ref[...] = jnp.zeros_like(choose_ref)
        gather_ref[...] = jnp.zeros_like(gather_ref)

    def wait_fetches():
        for k in range(chunks):
            fetch(k).wait()
        for load in loads:
            load.wait()

    for load in firsts:
        load.wait()
    if 0 == 1:
        for load in loads:
            load.start()
        wait_fetches()
        return stop(jnp.zeros((1, 128), f32))

    for b in range(PB_DEV):
        parts[b * ROWS : b * ROWS + 3, :] = parts_ref[:, b * BP : (b + 1) * BP].astype(f32)
    row = lax.broadcasted_iota(jnp.int32, (PB_DEV, slots), 0)
    chooser = jnp.where(row == part_ref[...], 1.0, 0.0).T.astype(bf16)
    tall = GROUP * 4
    for c in range(3):
        block = parts[pl.ds(c, PB_DEV, stride=ROWS), :].astype(bf16)
        got = dot(chooser, block)
        for i in range(GROUP):
            here = pl.ds(c * GROUP + i, groups, stride=tall)
            picks[here, :] = got[i * groups : (i + 1) * groups]
    if 0 == 2:
        wait_fetches()
        return stop(picks[0:1])
    if 0 == 3:
        wait_fetches()
    sub = lax.broadcasted_iota(jnp.int32, (tall, 128), 0) % GROUP
    half = lax.broadcasted_iota(jnp.int32, (tall, 128), 1) // BN
    low_slots = sub < 2
    own_half = sub % 2 == half
    for k in range(chunks):
        fetch(k).wait()
        if k == 0:
            for load in loads:
                load.start()
        for g in range(EDGES[k], EDGES[k + 1]):
            picked = picks[g * tall : (g + 1) * tall, :].astype(bf16)
            tiles = near_ref[:, g].reshape(GROUP * BN, BP)
            got = dot(picked, tiles, ((1,), (1,)))
            own = jnp.where(low_slots, got[:, :128], got[:, 128:])
            pairs[g * tall : (g + 1) * tall, :] = jnp.where(own_half, own, 0.0)
    if 0 == 3 or 0 == 4:
        for load in loads:
            load.wait()
        return stop(pairs[0:1])

    def pairs_of(c):
        return jnp.concatenate(
            [pairs[pl.ds(c * GROUP + i, groups, stride=tall), :] for i in range(GROUP)], axis=0
        )

    row = lax.broadcasted_iota(jnp.int32, (cells * per_row, slots), 0)
    block = row % cells * per_row + row // cells
    live = lax.broadcasted_iota(jnp.int32, (cells * per_row, slots), 1) < count[0]
    hits = jnp.where((block == node_ref[...]) & live, 1.0, 0.0)
    choose_ref[...] = hits.T.astype(bf16)
    hits = hits.astype(bf16)
    left = left_half((cells, 128))
    lines = []
    for c in range(3):
        total = dot(hits, jnp.concatenate(split(pairs_of(c)), axis=1))
        total = total[:, :128] + total[:, 128:]
        total += swap(total)
        pieces = [
            jnp.where(
                left, total[xb * cells : (xb + 1) * cells], total[(xb + 1) * cells : (xb + 2) * cells]
            )
            for xb in range(0, per_row, 2)
        ]
        lines.append(jnp.concatenate(pieces, axis=1))
    vort = jnp.concatenate([*lines, jnp.zeros((cells, NX), f32)], axis=0)
    loads[0].wait()
    if 0 == 5:
        for load in loads[1:]:
            load.wait()
        return stop(vort[0:1, 0:128])
    high, rest = split(vort)
    none = jnp.zeros_like(high)
    both = [
        jnp.concatenate(
            [jnp.concatenate([x, none], axis=1), jnp.concatenate([none, x], axis=1)], axis=0
        )
        for x in (high, rest)
    ]
    over = ((1,), (1,))
    modes = dot(x_ref[:, : 2 * NX], jnp.concatenate(both, axis=0), over)
    modes = modes[:, :128] + (modes[:, 128:] + dot(x_ref[:, 2 * NX :], both[0], over))
    send_a[...] = modes.reshape(MIDS, TALL, 128)
    pack(send_a, 0, MIDS)
    if 0 == 6:
        for load in loads[1:]:
            load.wait()
        return stop(send_a[0, 0:1])

    def push_modes(device):
        to_y, to_z = device
        push(send_a.at[(to_y - 1) * N_PZ + to_z], recv_a.at[me], 0, plane_sem.at[my_y], device)

    if not False:

        @pl.when(mid)
        def _():
            pl.semaphore_wait(barrier, devices - 1)

        @pl.when(outer)
        def _():
            pl.semaphore_wait(barrier, MIDS)

        for device in to_mids[:-1]:
            push_modes(device)

        @pl.when(outer)
        def _():
            push_modes(to_mids[-1])

    for load in loads[1:]:
        load.wait()
    recv_b[:, local:, :] = jnp.zeros((MIDS, TALL - local, 128), f32)
    row = lax.broadcasted_iota(jnp.int32, (PB_DEV, slots), 0)
    live = lax.broadcasted_iota(jnp.int32, (PB_DEV, slots), 1) < count[0]
    gather_ref[...] = jnp.where((row == part_ref[...]) & live, 1.0, 0.0).astype(bf16)

    def spread_out(i):
        return jnp.broadcast_to(small[i][:, None, :], (devices, TALL, 128)).reshape(rows, 128)

    sign = jnp.where(lax.broadcasted_iota(jnp.int32, (TALL, 128), 1) < 64, 1.0, -1.0)

    def ahead(x):
        return swap(x) * sign

    def astern(x):
        return swap(x) * -sign

    def along(x, table):
        return dot(jnp.concatenate(split(x), axis=1), table)

    def solve_modes():
        slot = lax.broadcasted_iota(jnp.int32, (rows, 128), 0) % TALL
        mode = my_mid * local + slot
        wave_x = mode.astype(f32) * (2.0 * math.pi / NX)
        total = spread_out(2) + wave_x * wave_x
        weight = jnp.where(mode == 0, 1.0, 2.0) * (1.0 / (NX * CY * N_PY * CZ * N_PZ))
        inverse = spread_out(7) * weight / jnp.where(total > 0, total, 1.0)
        held[0] = (spread_out(3) + wave_x * spread_out(5)) * inverse
        held[1] = (spread_out(4) + wave_x * spread_out(6)) * inverse
        held[2], held[3] = spread_out(0), spread_out(1)
        if False:
            recv_a[0:MIDS] = send_a[...]
            recv_a[MIDS:] = send_a[...]
        else:
            recv_a[me] = send_a[my_mid]
            recv_a[:, local:, :] = jnp.zeros((devices, TALL - local, 128), f32)
        planes = (
            (my_y, N_PZ - 1), (3 - my_y, N_PZ), (3 - opposite, N_PZ), (opposite, N_PZ)
        )
        for plane, many in planes:
            if not False:
                wait_blocks(recv_a, many, plane_sem.at[plane])
            first = plane * N_PZ
            unpack(recv_a, first, N_PZ)
            line = line_transform([recv_a[first + b] for b in range(N_PZ)], ahead)
            for b in range(N_PZ):
                recv_a[first + b] = line[b]
        if 0 == 7:
            return
        columns = [
            line_transform([recv_a[a * N_PZ + b] for a in range(N_PY)], ahead) for b in range(N_PZ)
        ]
        y = jnp.concatenate([columns[b][a] for a in range(N_PY) for b in range(N_PZ)], axis=0)
        z = held[2] * y + held[3] * swap(y)
        both = along(z, tab_ref[:, 0:256])
        vel = held[0] * both[:, :128] - held[1] * both[:, 128:]
        y = along(vel, tab_ref[:, 256:384])
        z = held[2] * y - held[3] * swap(y)
        z = [z[d * TALL : (d + 1) * TALL] for d in range(devices)]
        columns = [
            line_transform([z[a * N_PZ + b] for a in range(N_PY)], astern) for b in range(N_PZ)
        ]
        for plane in (0, 3, 1, 2):
            line = line_transform([columns[b][plane] for b in range(N_PZ)], astern)
            for b in range(N_PZ):
                send_b[plane * N_PZ + b] = line[b]
            pack(send_b, plane * N_PZ, N_PZ)
            if not False:
                for kz in PARTNERS[:-1]:
                    push_cells(plane, flip(my_z, kz))
                if plane in (0, 3):
                    push_cells(plane, my_z)
                else:
                    pl.when(my_y != plane)(functools.partial(push_cells, plane, my_z))
        recv_b[my_mid, 0:packed] = send_b[me, 0:packed]

    def push_cells(to_y, to_z):
        source = send_b.at[to_y * N_PZ + to_z]
        push(source, recv_b.at[my_mid], 1, recv_sem.at[1], (to_y, to_z))

    if False:
        solve_modes()
        if 0 == 7:
            return stop(recv_a[0, 0:1] + held[0, 0:1] + held[1, 0:1] + held[2, 0:1] + held[3, 0:1])
        if 0 == 11:
            return stop(send_b[0, 0:1])
    else:

        @pl.when(mid)
        def _():
            solve_modes()
            wait_blocks(send_a, MIDS - 1, send_sem.at[0])
            wait_blocks(recv_b, MIDS - 1, recv_sem.at[1])

        @pl.when(outer)
        def _():
            wait_blocks(send_a, MIDS, send_sem.at[0])
            wait_blocks(recv_b, MIDS, recv_sem.at[1])

    unpack(recv_b, 0, MIDS)
    back = recv_b[...].reshape(MIDS * TALL, 128).T
    grid = jnp.zeros((48, NX), f32)
    for k in range(2):
        high, rest = split(back[64 * k : 64 * k + 48])
        table = x_ref[:, k * NX : (k + 1) * NX]
        both = dot(jnp.concatenate([high, rest], axis=0), table)
        grid += both[:48] + (both[48:] + dot(high, x_ref[:, (k + 2) * NX : (k + 3) * NX]))
    if 0 == 12:
        return stop(grid[0:1, 0:128])
    for c in range(3):
        for xb in range(0, per_row, 2):
            piece = grid[c * cells : (c + 1) * cells, xb * BN : (xb + 2) * BN]
            other = swap(piece)
            for h, line in ((0, jnp.where(left, piece, other)), (1, jnp.where(left, other, piece))):
                vel_ref[c, (xb + h) * cells : (xb + h + 1) * cells, :] = line.astype(bf16)
    if not False:

        @pl.when(mid)
        def _():
            wait_blocks(send_b, devices - 1, send_sem.at[1])


def collect_kernel_b(vel_ref, choose_ref, gather_ref, w_ref, out_ref, picks, pairs, sums):
    groups = w_ref.shape[1]
    tall = GROUP * 4
    picks[...] = jnp.zeros_like(picks)
    chooser = choose_ref[...]
    for c in range(3):
        got = dot(chooser, vel_ref[c])
        for i in range(GROUP):
            here = pl.ds(c * GROUP + i, groups, stride=tall)
            picks[here, :] = got[i * groups : (i + 1) * groups]
    sub = lax.broadcasted_iota(jnp.int32, (tall, 128), 0) % GROUP
    half = lax.broadcasted_iota(jnp.int32, (tall, 128), 1) // BN
    first = (sub < 2) & (sub % 2 == half)
    second = (sub >= 2) & (sub % 2 == half)
    for g in range(groups):
        line = picks[g * tall : (g + 1) * tall, :]
        chosen = jnp.concatenate([jnp.where(first, line, 0.0), jnp.where(second, line, 0.0)], axis=1)
        pairs[g * tall : (g + 1) * tall, :] = dot(
            chosen.astype(bf16), w_ref[:, g].reshape(GROUP * BN, BP)
        )
    for c in range(3):
        lines = jnp.concatenate(
            [pairs[pl.ds(c * GROUP + i, groups, stride=tall), :] for i in range(GROUP)], axis=0
        )
        total = dot(gather_ref[...], jnp.concatenate(split(lines), axis=1))
        sums[pl.ds(c, PB_DEV, stride=ROWS), :] = total[:, :128] + total[:, 128:]
    for b in range(PB_DEV):
        out_ref[:, b * BP : (b + 1) * BP] = sums[b * ROWS : b * ROWS + 3, :]


def solve_direct(vort_p, weights, part, node, counts):
    devices = N_PY * N_PZ
    node_blocks = NX * CY * CZ // BN
    slots = weights.shape[0]
    groups = slots // GROUP
    vmem = pl.BlockSpec(memory_space=pltpu.VMEM)
    hbm = pl.BlockSpec(memory_space=pltpu.HBM)
    all_blocks, mid_blocks = (pltpu.VMEM((n, TALL, 128), f32) for n in (devices, MIDS))
    consts = [jnp.asarray(t) for t in tables()]
    weights = weights.reshape(GROUP, groups, BN, BP)
    inputs = [part[None], node[None], vort_p, weights, *consts]
    tall = pltpu.VMEM((groups * GROUP * 4, 128), f32)
    near, vel, chooser, gather = pl.pallas_call(
        solve_kernel,
        out_shape=(
            jax.ShapeDtypeStruct(weights.shape, weights.dtype),
            jax.ShapeDtypeStruct((3, node_blocks, 128), bf16),
            jax.ShapeDtypeStruct((slots, node_blocks), bf16),
            jax.ShapeDtypeStruct((PB_DEV, slots), bf16),
        ),
        in_specs=[pl.BlockSpec(memory_space=pltpu.SMEM)] + [hbm] * len(inputs),
        out_specs=(vmem, vmem, vmem, vmem),
        scratch_shapes=[
            pltpu.VMEM((1, slots), jnp.int32),
            pltpu.VMEM((1, slots), jnp.int32),
            pltpu.VMEM(vort_p.shape, vort_p.dtype),
            *[pltpu.VMEM(t.shape, t.dtype) for t in consts],
            mid_blocks,
            all_blocks,
            all_blocks,
            mid_blocks,
            pltpu.SemaphoreType.DMA((2,)),
            pltpu.SemaphoreType.DMA((2,)),
            pltpu.VMEM((PB_DEV * ROWS, BP), f32),
            tall,
            tall,
            pltpu.VMEM((4, devices * TALL, 128), f32),
            pltpu.SemaphoreType.DMA((2,)),
            pltpu.SemaphoreType.DMA((len(consts),)),
            pltpu.SemaphoreType.DMA((3,)),
            pltpu.SemaphoreType.DMA((N_PY,)),
        ],
        compiler_params=pltpu.CompilerParams(
            collective_id=None if False else 0, has_side_effects=True, vmem_limit_bytes=24 * 2**20
        ),
        name="solve",
    )(counts, *[pltpu.with_memory_space_constraint(x, pltpu.HBM) for x in inputs])
    return pl.pallas_call(
        collect_kernel_b,
        out_shape=jax.ShapeDtypeStruct((3, PB_DEV * BP), f32),
        in_specs=[vmem] * 4,
        out_specs=vmem,
        scratch_shapes=[tall, tall, pltpu.VMEM((PB_DEV * ROWS, BP), f32)],
        compiler_params=pltpu.CompilerParams(vmem_limit_bytes=16 * 2**20),
        name="collect_last",
    )(vel, chooser, gather, near)


def solve_staged(sums, n_py, n_pz):
    highest = lax.Precision.HIGHEST
    node_blocks = sums.shape[0]
    y_cells, z_cells = CY * n_py, CZ * n_pz
    x_modes = NX // 2
    sums = sums[:, :3, :BN] + sums[:, :3, BN:]
    vort_grid = sums.transpose(1, 0, 2).reshape(3, CZ, CY, NX)
    angle_fwd = twiddle(jnp.arange(NX), jnp.arange(x_modes), NX)
    x_forward = jnp.stack([jnp.cos(angle_fwd), -jnp.sin(angle_fwd)], 1)
    angle_inv = twiddle(jnp.arange(x_modes), jnp.arange(NX), NX)
    mode_weight = (jnp.where(jnp.arange(x_modes) == 0, 1.0, 2.0) / NX)[:, None]
    x_inverse = jnp.stack([mode_weight * jnp.cos(angle_inv), -mode_weight * jnp.sin(angle_inv)], 0)
    y_forward = forward_table(y_cells)
    z_forward = forward_table(z_cells)
    z_inverse = inverse_table(z_cells)
    y_inverse = inverse_table(y_cells)
    x_spectrum = jnp.einsum("czyx,xrm->czrmy", vort_grid, x_forward, precision=highest)
    row_section = jnp.einsum(
        "czrmy,rysk->cmskz",
        lax.all_to_all(x_spectrum, "py", split_axis=3, concat_axis=4, tiled=True),
        y_forward,
        precision=highest,
    )
    col_section = jnp.einsum(
        "cmrkz,rzsw->cmskw",
        lax.all_to_all(row_section, "pz", split_axis=3, concat_axis=4, tiled=True),
        z_forward,
        precision=highest,
    )
    vel_spectrum = curl_solve(col_section, y_cells, z_cells)
    z_back = jnp.einsum("cmrkw,rwsz->cmszk", vel_spectrum, z_inverse, precision=highest)
    y_back = jnp.einsum(
        "cmrzk,rksy->czsym",
        lax.all_to_all(z_back, "pz", split_axis=3, concat_axis=4, tiled=True),
        y_inverse,
        precision=highest,
    )
    vel_grid = jnp.einsum(
        "czrym,rmx->czyx",
        lax.all_to_all(y_back, "py", split_axis=3, concat_axis=4, tiled=True),
        x_inverse,
        precision=highest,
    )
    vel_nodes = vel_grid.astype(bf16).astype(f32).reshape(3, node_blocks, BN).transpose(1, 0, 2)
    vel_nodes = jnp.concatenate([vel_nodes, vel_nodes], axis=2)
    return jnp.pad(vel_nodes, ((0, 0), (0, ROWS - 3), (0, 0)))


def per_device(vort_p, pair_weights, pair_part, pair_node, counts):
    n_py, n_pz = lax.axis_size("py"), lax.axis_size("pz")
    node_blocks = NX * CY * CZ // BN
    if (n_py, n_pz) == (N_PY, N_PZ):
        return solve_direct(vort_p, pair_weights, pair_part, pair_node, counts)
    sums, near = spread(vort_p, pair_weights, pair_part, pair_node, counts, node_blocks)
    vel = solve_staged(sums, n_py, n_pz)
    return collect(vel, near, pair_part, pair_node, counts)


def solution(mesh):
    placed = (
        P(None, ("py", "pz")),
        P(("py", "pz"), None, None),
        P(("py", "pz")),
        P(("py", "pz")),
        P(("py", "pz")),
    )
    return jax.shard_map(
        per_device, mesh=mesh, in_specs=placed, out_specs=P(None, ("py", "pz")), check_vma=False
    )
```

```python
import functools
import math

import jax
import jax.numpy as jnp
import numpy as np
from jax import lax
from jax.experimental import pallas as pl
from jax.experimental.pallas import tpu as pltpu
from jax.sharding import PartitionSpec as P

NX = 384
CY = 8
CZ = 2
BP = 128
BN = 64
PB_DEV = 32
ROWS = 8
CHUNK = 32
GROUP = 4
N_PY = 4
N_PZ = 8
MESH = pl.DeviceIdType.MESH
f32 = jnp.float32
bf16 = jnp.bfloat16


def twiddle(row_index, col_index, period):
    product = row_index[:, None] * col_index[None, :] % period
    return product.astype(jnp.float32) * (2.0 * math.pi / period)


def forward_table(length):
    angle = twiddle(jnp.arange(length), jnp.arange(length), length)
    cosine = jnp.cos(angle)
    sines = jnp.sin(angle)
    return jnp.stack([jnp.stack([cosine, -sines], 1), jnp.stack([sines, cosine], 1)], 0)


def inverse_table(length):
    angle = twiddle(jnp.arange(length), jnp.arange(length), length)
    cosine = jnp.cos(angle) / length
    sines = jnp.sin(angle) / length
    return jnp.stack([jnp.stack([cosine, sines], 1), jnp.stack([-sines, cosine], 1)], 0)


def cross_terms(coeffs, field):
    return jnp.stack(
        [
            coeffs[1] * field[2] - coeffs[2] * field[1],
            coeffs[2] * field[0] - coeffs[0] * field[2],
            coeffs[0] * field[1] - coeffs[1] * field[0],
        ],
        axis=0,
    )


def signed_wave(length, index):
    signed = jnp.where(index < length // 2, index, index - length)
    return (signed.astype(jnp.float32) * (2.0 * math.pi / length), index == length // 2)


def curl_solve(spectrum, y_cells, z_cells):
    x_local = spectrum.shape[1]
    y_local = spectrum.shape[3]
    mode_x = lax.axis_index("py") * x_local + jnp.arange(x_local)
    wave_x = mode_x.astype(jnp.float32) * (2.0 * math.pi / NX)
    wave_y, edge_y = signed_wave(y_cells, lax.axis_index("pz") * y_local + jnp.arange(y_local))
    wave_z, edge_z = signed_wave(z_cells, jnp.arange(z_cells))
    wave_x3 = wave_x[:, None, None]
    wave_y3 = wave_y[None, :, None]
    wave_z3 = wave_z[None, None, :]
    total = wave_x3 * wave_x3 + wave_y3 * wave_y3 + wave_z3 * wave_z3
    edges = edge_y[None, :, None] | edge_z[None, None, :]
    keep = (total > 0) & jnp.logical_not(edges)
    inverse_sq = jnp.where(keep, 1.0 / jnp.where(keep, total, 1.0), 0.0)
    inv_wave = (wave_x3 * inverse_sq, wave_y3 * inverse_sq, wave_z3 * inverse_sq)
    real_turn = cross_terms(inv_wave, spectrum[:, :, 0])
    imag_turn = cross_terms(inv_wave, spectrum[:, :, 1])
    return jnp.stack([-imag_turn, real_turn], axis=2)


def halves(table):
    table = np.asarray(table, np.float32)
    high = table.astype(bf16)
    return high, (table - high.astype(np.float32)).astype(bf16)


def split(x):
    high = x.astype(bf16)
    return high, (x - high.astype(f32)).astype(bf16)


def dot(a, b, dims=((1,), (0,))):
    return lax.dot_general(a, b, (dims, ((), ())), preferred_element_type=f32)


def left_half(shape):
    return lax.broadcasted_iota(jnp.int32, shape, 1) < BN


def spread_kernel(part, node, count, parts_ref, w_ref, out_ref, near_ref, parts, sems):
    chunks = w_ref.shape[0] // CHUNK

    def fetch(k):
        here = pl.ds(k * CHUNK, CHUNK)
        return pltpu.make_async_copy(w_ref.at[here], near_ref.at[here], sems.at[k])

    for k in range(chunks):
        fetch(k).start()
    out_ref[...] = jnp.zeros_like(out_ref)
    parts[...] = jnp.zeros_like(parts)
    for b in range(PB_DEV):
        parts[b, 0:3, :] = parts_ref[:, b * BP : (b + 1) * BP].astype(f32)
    left = left_half((ROWS, 128))

    def chunk(k, carry):
        fetch(k).wait()
        base = k * CHUNK
        for g in range(CHUNK // GROUP):
            first = base + g * GROUP
            picked = jnp.concatenate([parts[part[first + i]] for i in range(GROUP)], axis=0)
            tiles = near_ref[pl.ds(first, GROUP)].reshape(GROUP * BN, BP)
            got = dot(picked.astype(bf16), tiles, ((1,), (1,)))
            for i in range(GROUP):
                keep = jnp.logical_and(left if i % 2 == 0 else ~left, first + i < count[0])
                lanes = i // 2 * 128
                own = got[i * ROWS : (i + 1) * ROWS, lanes : lanes + 128]
                out_ref[node[first + i]] += jnp.where(keep, own, 0.0)
        return carry

    lax.fori_loop(0, chunks, chunk, 0)


def spread(vort_p, weights, part, node, counts, node_blocks):
    smem = pl.BlockSpec(memory_space=pltpu.SMEM)
    vmem = pl.BlockSpec(memory_space=pltpu.VMEM)
    return pl.pallas_call(
        spread_kernel,
        out_shape=(
            jax.ShapeDtypeStruct((node_blocks, ROWS, 2 * BN), f32),
            jax.ShapeDtypeStruct(weights.shape, weights.dtype),
        ),
        in_specs=[smem, smem, smem, vmem, pl.BlockSpec(memory_space=pltpu.HBM)],
        out_specs=(vmem, vmem),
        scratch_shapes=[
            pltpu.VMEM((PB_DEV, ROWS, BP), f32),
            pltpu.SemaphoreType.DMA((weights.shape[0] // CHUNK,)),
        ],
        compiler_params=pltpu.CompilerParams(vmem_limit_bytes=48 * 2**20),
        name="spread",
    )(part, node, counts, vort_p, weights)


def collect_kernel(part, node, count, vel_ref, w_ref, out_ref, sums):
    sums[...] = jnp.zeros_like(sums)
    left = left_half((ROWS, 128))
    zero = jnp.zeros((ROWS, 128), f32)

    def chunk(k, carry):
        for g in range(CHUNK // GROUP):
            first = k * CHUNK + g * GROUP
            rows = []
            for i in range(GROUP):
                slot = first + i
                keep = jnp.logical_and(left if i % 2 == 0 else ~left, slot < count[0])
                own = jnp.where(keep, vel_ref[node[slot]], 0.0)
                rows.append(
                    jnp.concatenate(
                        [own if h == i // 2 else zero for h in range(GROUP // 2)], axis=1
                    )
                )
            chosen = jnp.concatenate(rows, axis=0).astype(bf16)
            got = dot(chosen, w_ref[pl.ds(first, GROUP)].reshape(GROUP * BN, BP))
            for i in range(GROUP):
                sums[part[first + i]] += got[i * ROWS : (i + 1) * ROWS]
        return carry

    lax.fori_loop(0, w_ref.shape[0] // CHUNK, chunk, 0)
    for b in range(PB_DEV):
        out_ref[:, b * BP : (b + 1) * BP] = sums[b, 0:3, :]


def collect(vel, weights, part, node, counts):
    smem = pl.BlockSpec(memory_space=pltpu.SMEM)
    vmem = pl.BlockSpec(memory_space=pltpu.VMEM)
    return pl.pallas_call(
        collect_kernel,
        out_shape=jax.ShapeDtypeStruct((3, PB_DEV * BP), f32),
        in_specs=[smem, smem, smem, vmem, vmem],
        out_specs=vmem,
        scratch_shapes=[pltpu.VMEM((PB_DEV, ROWS, BP), f32)],
        compiler_params=pltpu.CompilerParams(vmem_limit_bytes=24 * 2**20),
        name="collect",
    )(part, node, counts, vel, weights)


EDGES = (0, 28, 64)
MIDS = 2 * N_PZ
TALL = 16
PARTNERS = (6, 7, 4, 5, 2, 3, 1, 0)
HOPS = {0: 0, 1: 0, 2: 1, 3: 1, 4: 1, 5: 1, 6: 2, 7: 2}


def by_hops(planes):
    pairs = [(plane, kz) for plane in range(len(planes)) for kz in PARTNERS]
    return sorted(pairs, key=lambda pair: -(planes[pair[0]] + HOPS[pair[1]]))


def tables():
    devices = N_PY * N_PZ
    local = NX // 2 // MIDS
    ny, nz = CY * N_PY, CZ * N_PZ
    row = np.arange(MIDS * TALL)
    slot, device = row % TALL, row // TALL
    mode = device * local + slot
    angle = 2 * np.pi * (mode[:, None] * np.arange(NX)[None] % NX) / NX
    used = (slot < local)[:, None]
    x_cos, x_sin = np.where(used, np.cos(angle), 0.0), np.where(used, -np.sin(angle), 0.0)
    index = np.arange(devices)
    a, b = index // N_PZ, index % N_PZ
    lane = np.arange(128)
    real, comp, cell = lane // 64, lane % 64 // 16, lane % 16
    zl, yl = cell // CY, cell % CY
    valid = (comp < 3)[None]
    phi = 2 * np.pi * (a[:, None] * yl[None] / ny + b[:, None] * zl[None] / nz)
    sign = np.where(real == 0, 1.0, -1.0)[None]
    turn_cos, turn_sin = np.cos(phi), np.sin(phi) * sign
    psi = 2 * np.pi * (yl[:, None] * yl[None] / CY + zl[:, None] * zl[None] / CZ)
    cosine, sines = np.cos(psi), np.sin(psi)
    r, q = real[:, None], real[None]

    def near(ahead):
        both = np.where(r == q, sines, np.where(r == 0, cosine, -cosine))
        same = (comp[:, None] == (comp[None] + ahead) % 3) & (comp[:, None] < 3) & valid
        return np.where(same, both, 0.0)

    forward = np.concatenate([near(2), near(1)], 1)
    both = np.where(r == q, cosine, np.where(r == 0, sines, -sines))
    same = (comp[:, None] == comp[None]) & (comp[:, None] < 3)
    back = np.where(same, both, 0.0)
    my, mz = a[:, None] + N_PY * yl[None], b[:, None] + N_PZ * zl[None]
    keep = (my != ny // 2) & (mz != nz // 2) & valid
    my, mz = np.where(my < ny // 2, my, my - ny), np.where(mz < nz // 2, mz, mz - nz)
    ky, kz = 2 * np.pi * my / ny, 2 * np.pi * mz / nz
    zero = np.zeros_like(ky)
    wave = np.stack([zero, ky, kz])
    k_first = np.where(comp == 0, wave[1], np.where(comp == 1, wave[2], wave[0]))
    k_second = np.where(comp == 0, wave[2], np.where(comp == 1, wave[0], wave[1]))
    x_first = np.broadcast_to(comp == 2, ky.shape)
    x_second = np.broadcast_to(comp == 1, ky.shape)
    small = [turn_cos, turn_sin, ky * ky + kz * kz, k_first, k_second, x_first, x_second, keep]
    small = np.stack(small).astype(np.float32)
    near_table = np.concatenate([forward, back], 1)
    near_high = near_table.astype(np.float32).astype(bf16)
    return [
        np.concatenate(halves(np.concatenate([x_cos, x_sin], 1)), 1),
        np.concatenate([near_high, near_high], 0),
        small,
    ]


def flip(index, bits):
    for bit in (1, 2, 4):
        if bits & bit:
            index = index + bit - 2 * bit * (index // bit % 2)
    return index


def swap(x):
    return pltpu.roll(x, 64, 1)


def line_transform(x, turn):
    if len(x) == 2:
        return [x[0] + x[1], x[0] - x[1]]
    half = len(x) // 2
    even = [x[k] + x[k + half] for k in range(half)]
    odd = [x[k] - x[k + half] for k in range(half)]
    if half == 2:
        side = turn(odd[1])
        low, high = line_transform(even, turn), [odd[0] + side, odd[0] - side]
    else:
        side = turn(odd[2])
        near, far = odd[1] - odd[3], turn(odd[1] + odd[3])
        root = math.sqrt(0.5)
        plus, minus = (near + far) * root, (far - near) * root
        first, second = odd[0] + side, odd[0] - side
        low = line_transform(even, turn)
        high = [first + plus, second + minus, first - plus, second - minus]
    return [value for pair in zip(low, high) for value in pair]


def solve_kernel(
    count,
    part_hbm,
    node_hbm,
    parts_hbm,
    w_ref,
    x_hbm,
    near_hbm,
    small_hbm,
    near_ref,
    vel_ref,
    choose_ref,
    gather_ref,
    part_ref,
    node_ref,
    parts_ref,
    x_ref,
    tab_ref,
    small,
    send_a,
    recv_a,
    send_b,
    recv_b,
    send_sem,
    recv_sem,
    parts,
    picks,
    pairs,
    held,
    sems,
    const_sems,
    first_sems,
    plane_sem,
):
    devices = N_PY * N_PZ
    local = NX // 2 // MIDS
    rows = devices * TALL
    per_row = NX // BN
    cells = CY * CZ
    groups = w_ref.shape[1]
    slots = GROUP * groups
    chunks = sems.shape[0]
    my_y, my_z = lax.axis_index("py"), lax.axis_index("pz")
    me = my_y * N_PZ + my_z
    mid = (my_y == 1) | (my_y == 2)
    outer = jnp.logical_not(mid)
    my_mid = me - N_PZ
    near_plane, far_plane = 1 + my_y // 2, 2 - my_y // 2
    opposite = 6 - 3 * my_y
    mid_planes = (opposite, 3 - opposite, 3 - my_y, my_y)
    to_mids = [((far_plane, near_plane)[p], flip(my_z, kz)) for p, kz in by_hops((2, 1))]
    order = [pair for pair in by_hops((2, 1, 1, 0)) if pair != (3, 0)]
    to_all = [(mid_planes[p], flip(my_z, kz)) for p, kz in order]

    def fetch(k):
        here = pl.ds(EDGES[k], EDGES[k + 1] - EDGES[k])
        return pltpu.make_async_copy(w_ref.at[:, here], near_ref.at[:, here], sems.at[k])

    firsts = [
        pltpu.make_async_copy(c, h, first_sems.at[i])
        for i, (c, h) in enumerate(
            ((parts_hbm, parts_ref), (part_hbm, part_ref), (node_hbm, node_ref))
        )
    ]
    for load in firsts:
        load.start()
    for k in range(chunks):
        fetch(k).start()
    if not False:
        barrier = pltpu.get_barrier_semaphore()

        @pl.when(mid)
        def _():
            for other in to_all:
                pl.semaphore_signal(barrier, inc=1, device_id=other, device_id_type=MESH)

        @pl.when(outer)
        def _():
            for other in to_mids:
                pl.semaphore_signal(barrier, inc=1, device_id=other, device_id_type=MESH)

    loads = [
        pltpu.make_async_copy(c, h, const_sems.at[i])
        for i, (c, h) in enumerate(
            ((x_hbm, x_ref), (near_hbm, tab_ref), (small_hbm, small))
        )
    ]

    packed = 3 * local // 4
    sent = pl.ds(0, packed)
    spare = lax.broadcasted_iota(jnp.int32, (1, 128), 1) % 64 // 16

    def pack(buffer, first, many):
        lines = buffer.reshape(buffer.shape[0] * TALL, 128)
        for j in range(local - packed):
            extra = lines[pl.ds(first * TALL + packed + j, many, stride=TALL), :]
            for c in range(3):
                here = pl.ds(first * TALL + 3 * j + c, many, stride=TALL)
                moved = pltpu.roll(extra, 16 * (3 - c), 1)
                lines[here, :] = jnp.where(spare == 3, moved, lines[here, :])

    def unpack(buffer, first, many):
        lines = buffer.reshape(buffer.shape[0] * TALL, 128)
        for j in range(local - packed):
            extra = jnp.zeros((many, 128), f32)
            for c in range(3):
                line = lines[pl.ds(first * TALL + 3 * j + c, many, stride=TALL), :]
                moved = pltpu.roll(line, 128 - 16 * (3 - c), 1)
                extra = jnp.where(spare == c, moved, extra)
            lines[pl.ds(first * TALL + packed + j, many, stride=TALL), :] = extra

    def push(source, target, phase, landed, device):
        pltpu.make_async_remote_copy(
            src_ref=source.at[sent],
            dst_ref=target.at[sent],
            send_sem=send_sem.at[phase],
            recv_sem=landed,
            device_id=device,
            device_id_type=MESH,
        ).start()

    def wait_blocks(buffer, many, sem):
        blocks = buffer.at[pl.ds(0, many), sent]
        pltpu.make_async_copy(blocks, blocks, sem).wait()

    def stop(value):
        vel_ref[...] = jnp.zeros_like(vel_ref) + value.astype(bf16)
        choose_ref[...] = jnp.zeros_like(choose_ref)
        gather_ref[...] = jnp.zeros_like(gather_ref)

    def wait_fetches():
        for k in range(chunks):
            fetch(k).wait()
        for load in loads:
            load.wait()

    for load in firsts:
        load.wait()
    if 0 == 1:
        for load in loads:
            load.start()
        wait_fetches()
        return stop(jnp.zeros((1, 128), f32))

    for b in range(PB_DEV):
        parts[b * ROWS : b * ROWS + 3, :] = parts_ref[:, b * BP : (b + 1) * BP].astype(f32)
    row = lax.broadcasted_iota(jnp.int32, (PB_DEV, slots), 0)
    chooser = jnp.where(row == part_ref[...], 1.0, 0.0).T.astype(bf16)
    tall = GROUP * 4
    for c in range(3):
        block = parts[pl.ds(c, PB_DEV, stride=ROWS), :].astype(bf16)
        got = dot(chooser, block)
        for i in range(GROUP):
            here = pl.ds(c * GROUP + i, groups, stride=tall)
            picks[here, :] = got[i * groups : (i + 1) * groups]
    if 0 == 2:
        wait_fetches()
        return stop(picks[0:1])
    if 0 == 3:
        wait_fetches()
    sub = lax.broadcasted_iota(jnp.int32, (tall, 128), 0) % GROUP
    half = lax.broadcasted_iota(jnp.int32, (tall, 128), 1) // BN
    low_slots = sub < 2
    own_half = sub % 2 == half
    for k in range(chunks):
        fetch(k).wait()
        if k == 0:
            for load in loads:
                load.start()
        for g in range(EDGES[k], EDGES[k + 1]):
            picked = picks[g * tall : (g + 1) * tall, :].astype(bf16)
            tiles = near_ref[:, g].reshape(GROUP * BN, BP)
            got = dot(picked, tiles, ((1,), (1,)))
            own = jnp.where(low_slots, got[:, :128], got[:, 128:])
            pairs[g * tall : (g + 1) * tall, :] = jnp.where(own_half, own, 0.0)
    if 0 == 3 or 0 == 4:
        for load in loads:
            load.wait()
        return stop(pairs[0:1])

    def pairs_of(c):
        return jnp.concatenate(
            [pairs[pl.ds(c * GROUP + i, groups, stride=tall), :] for i in range(GROUP)], axis=0
        )

    row = lax.broadcasted_iota(jnp.int32, (cells * per_row, slots), 0)
    block = row % cells * per_row + row // cells
    live = lax.broadcasted_iota(jnp.int32, (cells * per_row, slots), 1) < count[0]
    hits = jnp.where((block == node_ref[...]) & live, 1.0, 0.0)
    choose_ref[...] = hits.T.astype(bf16)
    hits = hits.astype(bf16)
    left = left_half((cells, 128))
    lines = []
    for c in range(3):
        total = dot(hits, jnp.concatenate(split(pairs_of(c)), axis=1))
        total = total[:, :128] + total[:, 128:]
        total += swap(total)
        pieces = [
            jnp.where(
                left, total[xb * cells : (xb + 1) * cells], total[(xb + 1) * cells : (xb + 2) * cells]
            )
            for xb in range(0, per_row, 2)
        ]
        lines.append(jnp.concatenate(pieces, axis=1))
    vort = jnp.concatenate([*lines, jnp.zeros((cells, NX), f32)], axis=0)
    loads[0].wait()
    if 0 == 5:
        for load in loads[1:]:
            load.wait()
        return stop(vort[0:1, 0:128])
    high, rest = split(vort)
    none = jnp.zeros_like(high)
    both = [
        jnp.concatenate(
            [jnp.concatenate([x, none], axis=1), jnp.concatenate([none, x], axis=1)], axis=0
        )
        for x in (high, rest)
    ]
    over = ((1,), (1,))
    modes = dot(x_ref[:, : 2 * NX], jnp.concatenate(both, axis=0), over)
    modes = modes[:, :128] + (modes[:, 128:] + dot(x_ref[:, 2 * NX :], both[0], over))
    send_a[...] = modes.reshape(MIDS, TALL, 128)
    pack(send_a, 0, MIDS)
    if 0 == 6:
        for load in loads[1:]:
            load.wait()
        return stop(send_a[0, 0:1])

    def push_modes(device):
        to_y, to_z = device
        push(send_a.at[(to_y - 1) * N_PZ + to_z], recv_a.at[me], 0, plane_sem.at[my_y], device)

    if not False:

        @pl.when(mid)
        def _():
            pl.semaphore_wait(barrier, devices - 1)

        @pl.when(outer)
        def _():
            pl.semaphore_wait(barrier, MIDS)

        for device in to_mids[:-1]:
            push_modes(device)

        @pl.when(outer)
        def _():
            push_modes(to_mids[-1])

    for load in loads[1:]:
        load.wait()
    recv_b[:, local:, :] = jnp.zeros((MIDS, TALL - local, 128), f32)
    row = lax.broadcasted_iota(jnp.int32, (PB_DEV, slots), 0)
    live = lax.broadcasted_iota(jnp.int32, (PB_DEV, slots), 1) < count[0]
    gather_ref[...] = jnp.where((row == part_ref[...]) & live, 1.0, 0.0).astype(bf16)

    def spread_out(i):
        return jnp.broadcast_to(small[i][:, None, :], (devices, TALL, 128)).reshape(rows, 128)

    sign = jnp.where(lax.broadcasted_iota(jnp.int32, (TALL, 128), 1) < 64, 1.0, -1.0)

    def ahead(x):
        return swap(x) * sign

    def astern(x):
        return swap(x) * -sign

    def along(x, table):
        return dot(jnp.concatenate(split(x), axis=1), table)

    def solve_modes():
        slot = lax.broadcasted_iota(jnp.int32, (rows, 128), 0) % TALL
        mode = my_mid * local + slot
        wave_x = mode.astype(f32) * (2.0 * math.pi / NX)
        total = spread_out(2) + wave_x * wave_x
        weight = jnp.where(mode == 0, 1.0, 2.0) * (1.0 / (NX * CY * N_PY * CZ * N_PZ))
        inverse = spread_out(7) * weight / jnp.where(total > 0, total, 1.0)
        held[0] = (spread_out(3) + wave_x * spread_out(5)) * inverse
        held[1] = (spread_out(4) + wave_x * spread_out(6)) * inverse
        held[2], held[3] = spread_out(0), spread_out(1)
        if False:
            recv_a[0:MIDS] = send_a[...]
            recv_a[MIDS:] = send_a[...]
        else:
            recv_a[me] = send_a[my_mid]
            recv_a[:, local:, :] = jnp.zeros((devices, TALL - local, 128), f32)
        planes = (
            (my_y, N_PZ - 1), (3 - my_y, N_PZ), (3 - opposite, N_PZ), (opposite, N_PZ)
        )
        for plane, many in planes:
            if not False:
                wait_blocks(recv_a, many, plane_sem.at[plane])
            first = plane * N_PZ
            unpack(recv_a, first, N_PZ)
            line = line_transform([recv_a[first + b] for b in range(N_PZ)], ahead)
            for b in range(N_PZ):
                recv_a[first + b] = line[b]
        if 0 == 7:
            return
        columns = [
            line_transform([recv_a[a * N_PZ + b] for a in range(N_PY)], ahead) for b in range(N_PZ)
        ]
        y = jnp.concatenate([columns[b][a] for a in range(N_PY) for b in range(N_PZ)], axis=0)
        z = held[2] * y + held[3] * swap(y)
        both = along(z, tab_ref[:, 0:256])
        vel = held[0] * both[:, :128] - held[1] * both[:, 128:]
        y = along(vel, tab_ref[:, 256:384])
        z = held[2] * y - held[3] * swap(y)
        z = [z[d * TALL : (d + 1) * TALL] for d in range(devices)]
        columns = [
            line_transform([z[a * N_PZ + b] for a in range(N_PY)], astern) for b in range(N_PZ)
        ]
        for plane in (0, 3, 1, 2):
            line = line_transform([columns[b][plane] for b in range(N_PZ)], astern)
            for b in range(N_PZ):
                send_b[plane * N_PZ + b] = line[b]
            pack(send_b, plane * N_PZ, N_PZ)
            if not False:
                if plane == 0:
                    for to_z in range(N_PZ):
                        push_cells(plane, to_z)
                    continue
                for kz in PARTNERS[:-1]:
                    push_cells(plane, flip(my_z, kz))
                if plane in (0, 3):
                    push_cells(plane, my_z)
                else:
                    pl.when(my_y != plane)(functools.partial(push_cells, plane, my_z))
        recv_b[my_mid, 0:packed] = send_b[me, 0:packed]

    def push_cells(to_y, to_z):
        source = send_b.at[to_y * N_PZ + to_z]
        push(source, recv_b.at[my_mid], 1, recv_sem.at[1], (to_y, to_z))

    if False:
        solve_modes()
        if 0 == 7:
            return stop(recv_a[0, 0:1] + held[0, 0:1] + held[1, 0:1] + held[2, 0:1] + held[3, 0:1])
        if 0 == 11:
            return stop(send_b[0, 0:1])
    else:

        @pl.when(mid)
        def _():
            solve_modes()
            wait_blocks(send_a, MIDS - 1, send_sem.at[0])
            wait_blocks(recv_b, MIDS - 1, recv_sem.at[1])

        @pl.when(outer)
        def _():
            wait_blocks(send_a, MIDS, send_sem.at[0])
            wait_blocks(recv_b, MIDS, recv_sem.at[1])

    unpack(recv_b, 0, MIDS)
    back = recv_b[...].reshape(MIDS * TALL, 128).T
    grid = jnp.zeros((48, NX), f32)
    for k in range(2):
        high, rest = split(back[64 * k : 64 * k + 48])
        table = x_ref[:, k * NX : (k + 1) * NX]
        both = dot(jnp.concatenate([high, rest], axis=0), table)
        grid += both[:48] + (both[48:] + dot(high, x_ref[:, (k + 2) * NX : (k + 3) * NX]))
    if 0 == 12:
        return stop(grid[0:1, 0:128])
    for c in range(3):
        for xb in range(0, per_row, 2):
            piece = grid[c * cells : (c + 1) * cells, xb * BN : (xb + 2) * BN]
            other = swap(piece)
            for h, line in ((0, jnp.where(left, piece, other)), (1, jnp.where(left, other, piece))):
                vel_ref[c, (xb + h) * cells : (xb + h + 1) * cells, :] = line.astype(bf16)
    if not False:

        @pl.when(mid)
        def _():
            wait_blocks(send_b, devices - 1, send_sem.at[1])


def collect_kernel_b(vel_ref, choose_ref, gather_ref, w_ref, out_ref, picks, pairs, sums):
    groups = w_ref.shape[1]
    tall = GROUP * 4
    picks[...] = jnp.zeros_like(picks)
    chooser = choose_ref[...]
    for c in range(3):
        got = dot(chooser, vel_ref[c])
        for i in range(GROUP):
            here = pl.ds(c * GROUP + i, groups, stride=tall)
            picks[here, :] = got[i * groups : (i + 1) * groups]
    sub = lax.broadcasted_iota(jnp.int32, (tall, 128), 0) % GROUP
    half = lax.broadcasted_iota(jnp.int32, (tall, 128), 1) // BN
    first = (sub < 2) & (sub % 2 == half)
    second = (sub >= 2) & (sub % 2 == half)
    for g in range(groups):
        line = picks[g * tall : (g + 1) * tall, :]
        chosen = jnp.concatenate([jnp.where(first, line, 0.0), jnp.where(second, line, 0.0)], axis=1)
        pairs[g * tall : (g + 1) * tall, :] = dot(
            chosen.astype(bf16), w_ref[:, g].reshape(GROUP * BN, BP)
        )
    for c in range(3):
        lines = jnp.concatenate(
            [pairs[pl.ds(c * GROUP + i, groups, stride=tall), :] for i in range(GROUP)], axis=0
        )
        total = dot(gather_ref[...], jnp.concatenate(split(lines), axis=1))
        sums[pl.ds(c, PB_DEV, stride=ROWS), :] = total[:, :128] + total[:, 128:]
    for b in range(PB_DEV):
        out_ref[:, b * BP : (b + 1) * BP] = sums[b * ROWS : b * ROWS + 3, :]


def solve_direct(vort_p, weights, part, node, counts):
    devices = N_PY * N_PZ
    node_blocks = NX * CY * CZ // BN
    slots = weights.shape[0]
    groups = slots // GROUP
    vmem = pl.BlockSpec(memory_space=pltpu.VMEM)
    hbm = pl.BlockSpec(memory_space=pltpu.HBM)
    all_blocks, mid_blocks = (pltpu.VMEM((n, TALL, 128), f32) for n in (devices, MIDS))
    consts = [jnp.asarray(t) for t in tables()]
    weights = weights.reshape(GROUP, groups, BN, BP)
    inputs = [part[None], node[None], vort_p, weights, *consts]
    tall = pltpu.VMEM((groups * GROUP * 4, 128), f32)
    near, vel, chooser, gather = pl.pallas_call(
        solve_kernel,
        out_shape=(
            jax.ShapeDtypeStruct(weights.shape, weights.dtype),
            jax.ShapeDtypeStruct((3, node_blocks, 128), bf16),
            jax.ShapeDtypeStruct((slots, node_blocks), bf16),
            jax.ShapeDtypeStruct((PB_DEV, slots), bf16),
        ),
        in_specs=[pl.BlockSpec(memory_space=pltpu.SMEM)] + [hbm] * len(inputs),
        out_specs=(vmem, vmem, vmem, vmem),
        scratch_shapes=[
            pltpu.VMEM((1, slots), jnp.int32),
            pltpu.VMEM((1, slots), jnp.int32),
            pltpu.VMEM(vort_p.shape, vort_p.dtype),
            *[pltpu.VMEM(t.shape, t.dtype) for t in consts],
            mid_blocks,
            all_blocks,
            all_blocks,
            mid_blocks,
            pltpu.SemaphoreType.DMA((2,)),
            pltpu.SemaphoreType.DMA((2,)),
            pltpu.VMEM((PB_DEV * ROWS, BP), f32),
            tall,
            tall,
            pltpu.VMEM((4, devices * TALL, 128), f32),
            pltpu.SemaphoreType.DMA((2,)),
            pltpu.SemaphoreType.DMA((len(consts),)),
            pltpu.SemaphoreType.DMA((3,)),
            pltpu.SemaphoreType.DMA((N_PY,)),
        ],
        compiler_params=pltpu.CompilerParams(
            collective_id=None if False else 0, has_side_effects=True, vmem_limit_bytes=24 * 2**20
        ),
        name="solve",
    )(counts, *[pltpu.with_memory_space_constraint(x, pltpu.HBM) for x in inputs])
    return pl.pallas_call(
        collect_kernel_b,
        out_shape=jax.ShapeDtypeStruct((3, PB_DEV * BP), f32),
        in_specs=[vmem] * 4,
        out_specs=vmem,
        scratch_shapes=[tall, tall, pltpu.VMEM((PB_DEV * ROWS, BP), f32)],
        compiler_params=pltpu.CompilerParams(vmem_limit_bytes=16 * 2**20),
        name="collect_last",
    )(vel, chooser, gather, near)


def solve_staged(sums, n_py, n_pz):
    highest = lax.Precision.HIGHEST
    node_blocks = sums.shape[0]
    y_cells, z_cells = CY * n_py, CZ * n_pz
    x_modes = NX // 2
    sums = sums[:, :3, :BN] + sums[:, :3, BN:]
    vort_grid = sums.transpose(1, 0, 2).reshape(3, CZ, CY, NX)
    angle_fwd = twiddle(jnp.arange(NX), jnp.arange(x_modes), NX)
    x_forward = jnp.stack([jnp.cos(angle_fwd), -jnp.sin(angle_fwd)], 1)
    angle_inv = twiddle(jnp.arange(x_modes), jnp.arange(NX), NX)
    mode_weight = (jnp.where(jnp.arange(x_modes) == 0, 1.0, 2.0) / NX)[:, None]
    x_inverse = jnp.stack([mode_weight * jnp.cos(angle_inv), -mode_weight * jnp.sin(angle_inv)], 0)
    y_forward = forward_table(y_cells)
    z_forward = forward_table(z_cells)
    z_inverse = inverse_table(z_cells)
    y_inverse = inverse_table(y_cells)
    x_spectrum = jnp.einsum("czyx,xrm->czrmy", vort_grid, x_forward, precision=highest)
    row_section = jnp.einsum(
        "czrmy,rysk->cmskz",
        lax.all_to_all(x_spectrum, "py", split_axis=3, concat_axis=4, tiled=True),
        y_forward,
        precision=highest,
    )
    col_section = jnp.einsum(
        "cmrkz,rzsw->cmskw",
        lax.all_to_all(row_section, "pz", split_axis=3, concat_axis=4, tiled=True),
        z_forward,
        precision=highest,
    )
    vel_spectrum = curl_solve(col_section, y_cells, z_cells)
    z_back = jnp.einsum("cmrkw,rwsz->cmszk", vel_spectrum, z_inverse, precision=highest)
    y_back = jnp.einsum(
        "cmrzk,rksy->czsym",
        lax.all_to_all(z_back, "pz", split_axis=3, concat_axis=4, tiled=True),
        y_inverse,
        precision=highest,
    )
    vel_grid = jnp.einsum(
        "czrym,rmx->czyx",
        lax.all_to_all(y_back, "py", split_axis=3, concat_axis=4, tiled=True),
        x_inverse,
        precision=highest,
    )
    vel_nodes = vel_grid.astype(bf16).astype(f32).reshape(3, node_blocks, BN).transpose(1, 0, 2)
    vel_nodes = jnp.concatenate([vel_nodes, vel_nodes], axis=2)
    return jnp.pad(vel_nodes, ((0, 0), (0, ROWS - 3), (0, 0)))


def per_device(vort_p, pair_weights, pair_part, pair_node, counts):
    n_py, n_pz = lax.axis_size("py"), lax.axis_size("pz")
    node_blocks = NX * CY * CZ // BN
    if (n_py, n_pz) == (N_PY, N_PZ):
        return solve_direct(vort_p, pair_weights, pair_part, pair_node, counts)
    sums, near = spread(vort_p, pair_weights, pair_part, pair_node, counts, node_blocks)
    vel = solve_staged(sums, n_py, n_pz)
    return collect(vel, near, pair_part, pair_node, counts)


def solution(mesh):
    placed = (
        P(None, ("py", "pz")),
        P(("py", "pz"), None, None),
        P(("py", "pz")),
        P(("py", "pz")),
        P(("py", "pz")),
    )
    return jax.shard_map(
        per_device, mesh=mesh, in_specs=placed, out_specs=P(None, ("py", "pz")), check_vma=False
    )
```
